512 devices in a mesh: gx: 128 (over y_hi, z, x), gy: 4 (over y_lo, core).
Axes of the slice: x: 4, y: 8 (y_hi: 4, y_lo: 2; y = y_hi * 2 + y_lo), z: 8, core: 2. Of those that a mesh axis runs over, the one named last changes fastest.
Arguments:
- unknown: float32 [2, 1024, 4096], P(None, 'gx', 'gy'), may hold values from -6 to 6
- height: float32 [1024, 4096], P('gx', 'gy'), may hold values from -0.4 to 0.4
- spectrum_flat: float32 [2, 4194304], P(None, ('gx', 'gy')), may hold values from -1.5 to 1.5
- spectrum_slope: float32 [2, 4194304], P(None, ('gx', 'gy')), may hold values from -15 to 15
- spectrum_curve: float32 [2, 4194304], P(None, ('gx', 'gy')), may hold values from -150 to 150
Outputs:
- applied: float32 [2, 1024, 4096], P(None, 'gx', 'gy')
The draws below stay inside these ranges and needn't reach their ends.
All inputs are finite; a program needn't handle non-finite values.
Results may differ from the reference program's by a relative error of at most 0.0001.
Values sent between devices are 32-bit elements; how exact they have to be, the bound alone decides.
No kernel may reach another device: no remote copies, remote signals or barrier semaphores. Data moves between devices by JAX's collectives and lax.ppermute only.
A program may use at most 128 MiB of HBM per device.

```python
import math
import jax
import jax.numpy as jnp
from jax import lax

ROWS_DEV = 8
NY = 4096
TILE = 4
NX = 1024
N_GX = 128
N_GY = 4


def level_of(stream_key, extent, shards, smallest, high):
    loudness, own = 1.0, jax.random.fold_in(stream_key, 6)
    for position, shards_of in shards:
        heights = jnp.exp(jax.random.uniform(jax.random.fold_in(own, position), (shards_of,), jnp.float32, smallest / len(shards), high / len(shards)))
        loudness = loudness * jnp.repeat(heights, extent[position] // shards_of).reshape([-1 if axis == position else 1 for axis in range(len(extent))])
    return loudness


def normal_values(rng, shape, spread, most, shards=(), held_as=jnp.bfloat16):
    loudness = level_of(rng, shape, shards, -0.22, 0.18) if shards else 1.0
    values = jax.random.normal(rng, shape, jnp.float32) * spread * loudness
    return jnp.minimum(jnp.maximum(values, -most), most).astype(held_as)


def setup_inputs(seed: int = 0) -> dict:
    seeds = jax.random.split(jax.random.key(seed), 6)
    return {
        "unknown": normal_values(seeds[0], (2, NX, NY), 1.0, 6.0, ((1, 128), (2, 4)), jnp.float32),
        "height": normal_values(seeds[1], (NX, NY), 0.08, 0.4, ((0, 128), (1, 4)), jnp.float32),
        "spectrum_flat": normal_values(seeds[2], (2, NX * NY), 0.25, 1.5, ((1, 512),), jnp.float32),
        "spectrum_slope": normal_values(seeds[3], (2, NX * NY), 2.5, 15.0, ((1, 512),), jnp.float32),
        "spectrum_curve": normal_values(seeds[4], (2, NX * NY), 25.0, 150.0, ((1, 512),), jnp.float32),
    }


wave_number = 2.0 * math.pi
spacing = 0.1
lift_height = 0.05
area_weight = spacing * spacing
neighbour_shifts = ((0, 0), (-1, 0), (1, 0), (0, -1), (0, 1))
mixing = ((1.0, -1.0, 1.0), (1.0, -2.0), (1.0,))

def offset_tables(tile_side):
    tile_cells = jnp.arange(tile_side * tile_side, dtype=jnp.int32)
    cell_row = tile_cells // tile_side
    cell_col = tile_cells % tile_side
    tables = []
    for shift_row, shift_col in neighbour_shifts:
        delta_row = (tile_side * shift_row + cell_row[None, :] - cell_row[:, None]).astype(jnp.float32)
        delta_col = (tile_side * shift_col + cell_col[None, :] - cell_col[:, None]).astype(jnp.float32)
        tables.append(spacing * spacing * (delta_row * delta_row + delta_col * delta_col))
    return tables

def flat_terms(distance_sq):
    radius = jnp.sqrt(distance_sq + lift_height * lift_height)
    inverse = 1.0 / radius
    green_real = jnp.cos(wave_number * radius) * inverse
    green_imag = jnp.sin(wave_number * radius) * inverse
    first_real = -lift_height * inverse * inverse
    first_imag = wave_number * lift_height * inverse
    lift_ratio = lift_height * lift_height * inverse * inverse
    second_real = (inverse * inverse - wave_number * wave_number) * lift_ratio + lift_ratio * inverse * inverse - inverse * (inverse - lift_ratio * inverse)
    second_imag = -2.0 * wave_number * inverse * lift_ratio + wave_number * (inverse - lift_ratio * inverse)
    slope_real = green_real * first_real - green_imag * first_imag
    slope_imag = green_real * first_imag + green_imag * first_real
    curve_real = 0.5 * (green_real * second_real - green_imag * second_imag)
    curve_imag = 0.5 * (green_real * second_imag + green_imag * second_real)
    return (green_real, green_imag, slope_real, slope_imag, curve_real, curve_imag)

def near_block(sources, observer_height, tables, flat_coeffs):
    total_real = jnp.zeros(observer_height.shape, observer_height.dtype)
    total_imag = jnp.zeros(observer_height.shape, observer_height.dtype)
    for neighbour in range(5):
        height_gap = observer_height[:, None, :] - sources[neighbour, 2][None, :, :]
        distance_sq = tables[neighbour][:, :, None]
        coeffs = [coefficient[:, :, None] for coefficient in flat_coeffs[neighbour]]
        lifted = lift_height + height_gap
        radius = jnp.sqrt(distance_sq + lifted * lifted)
        inverse = 1.0 / radius
        corr_real = jnp.cos(wave_number * radius) * inverse - (coeffs[0] + coeffs[2] * height_gap + coeffs[4] * height_gap * height_gap)
        corr_imag = jnp.sin(wave_number * radius) * inverse - (coeffs[1] + coeffs[3] * height_gap + coeffs[5] * height_gap * height_gap)
        source_real = sources[neighbour, 0][None, :, :]
        source_imag = sources[neighbour, 1][None, :, :]
        total_real = total_real + lax.optimization_barrier(jnp.sum(corr_real * source_real - corr_imag * source_imag, axis=1))
        total_imag = total_imag + lax.optimization_barrier(jnp.sum(corr_real * source_imag + corr_imag * source_real, axis=1))
    return jnp.stack([total_real, total_imag])

def tiled_near(sources, tile_side, block_size):
    tile_cells = tile_side * tile_side
    tile_count = sources.shape[3]
    step_count = tile_count // block_size
    tables = offset_tables(tile_side)
    flat_coeffs = [flat_terms(table) for table in tables]
    grouped = sources.reshape(5, 3, tile_cells, step_count, block_size).transpose(3, 0, 1, 2, 4)

    def apply_block(tile_block):
        return near_block(tile_block, tile_block[0, 2], tables, flat_coeffs)
    results = lax.map(apply_block, grouped)
    return results.transpose(1, 2, 0, 3).reshape(2, tile_cells, tile_count)

def tile_grid(values, tile_side):
    components, length, breadth = values.shape
    blocks = values.reshape(components, length // tile_side, tile_side, breadth // tile_side, tile_side)
    return blocks.transpose(0, 2, 4, 1, 3).reshape(components, tile_side * tile_side, length // tile_side, breadth // tile_side)

def untile(tiles, tile_side):
    components, tile_cells, tile_rows, tile_cols = tiles.shape
    blocks = tiles.reshape(components, tile_side, tile_side, tile_rows, tile_cols)
    return blocks.transpose(0, 3, 1, 4, 2).reshape(components, tile_rows * tile_side, tile_cols * tile_side)

def natural_spectrum(spectrum):
    narrow = NY // (N_GX * N_GY)
    blocks = spectrum.reshape(2, N_GX, N_GY, N_GX, ROWS_DEV, narrow)
    ordered = blocks.transpose(0, 4, 3, 1, 5, 2).reshape(2, NX, NY)
    return ordered[0] + 1j * ordered[1]

def reference(unknown, height, spectrum_flat, spectrum_slope, spectrum_curve):
    surface_field = unknown[0] + 1j * unknown[1]
    kernels = [natural_spectrum(spectrum_flat), natural_spectrum(spectrum_slope), natural_spectrum(spectrum_curve)]
    moments = [surface_field, height * surface_field, height * height * surface_field]
    transforms = [jnp.fft.fft2(moment) for moment in moments]
    far_part = jnp.zeros_like(surface_field)
    for degree in range(3):
        mixed_sum = jnp.zeros_like(surface_field)
        for source in range(3 - degree):
            mixed_sum = mixed_sum + mixing[degree][source] * kernels[degree + source] * transforms[source]
        far_part = far_part + height ** degree * jnp.fft.ifft2(mixed_sum)
    stacked = jnp.stack([unknown[0], unknown[1], height])
    tile_view = tile_grid(stacked, TILE)
    neighbours = [tile_view, jnp.roll(tile_view, 1, 2), jnp.roll(tile_view, -1, 2), jnp.roll(tile_view, 1, 3), jnp.roll(tile_view, -1, 3)]
    tile_rows = tile_view.shape[2]
    tile_cols = tile_view.shape[3]
    tile_count = tile_rows * tile_cols
    sources = jnp.stack(neighbours).reshape(5, 3, TILE * TILE, tile_count)
    block_size = 1024 if tile_count % 1024 == 0 else tile_count
    near_part = untile(tiled_near(sources, TILE, block_size).reshape(2, TILE * TILE, tile_rows, tile_cols), TILE)
    total_real = jnp.real(far_part) + area_weight * near_part[0]
    total_imag = jnp.imag(far_part) + area_weight * near_part[1]
    return jnp.stack([total_real, total_imag]).astype(jnp.float32)
```

```python
import functools
import math

import jax
import jax.numpy as jnp
import numpy as np
from jax import lax
from jax.experimental import pallas as pl
from jax.experimental.pallas import tpu as pltpu
from jax.sharding import PartitionSpec as P

TILE = 4
wave_number = 2.0 * math.pi
spacing = 0.1
lift_height = 0.05
area_weight = spacing * spacing
highest = lax.Precision.HIGHEST

ROWS = 8
SPAN = 1024
DEV_X = 128
DEV_Y = 4
LANES = 128
SUBS = SPAN // LANES
NARROW = 8
NX = ROWS * DEV_X
NY = SPAN * DEV_Y
HALF = ROWS * NARROW


def real_form(coeff):
    return np.block([[coeff.real, -coeff.imag], [coeff.imag, coeff.real]])


def make_tables():
    r8 = np.arange(8)
    lane = np.arange(LANES)
    eye = np.eye(8)
    row_first, row_twist, back_twist, back_last = [], [], [], []
    for q in range(DEV_Y):
        small = np.exp(-2j * np.pi * (np.outer(r8, r8) / 8 + r8[None, :] * q / 32))
        grown = np.einsum("cn,rs->rcns", small, eye).reshape(HALF, HALF)
        row_first.append(real_form(grown))
        phase = np.exp(-2j * np.pi * lane[None, :] * (r8[:, None] / 1024 + q / 4096))
        phase = np.tile(phase, (8, 1))
        row_twist.append(np.stack([phase.real, phase.imag]))
        turn = phase.conj().T
        back_twist.append(
            np.stack(
                [
                    np.concatenate([turn.real, turn.real], 1),
                    np.concatenate([-turn.imag, turn.imag], 1),
                ]
            )
        )
        wide = np.einsum("cn,rs->nrsc", small.conj(), eye).reshape(HALF, HALF)
        back_last.append(real_form(wide))
    ring = 2 * np.pi * np.outer(lane, lane) / LANES
    outer = np.concatenate([np.cos(ring), np.sin(ring)], 1)
    turn = np.exp(-2j * np.pi * np.outer(lane, np.repeat(r8, NARROW)) / NX)
    col_twist = np.stack(
        [
            np.concatenate([turn.real, turn.real], 1),
            np.concatenate([-turn.imag, turn.imag], 1),
        ]
    )
    ring8 = np.exp(-2j * np.pi * np.outer(r8, r8) / 8)
    grown = np.kron(ring8, np.eye(NARROW))
    col_small = real_form(grown).T
    col_back = real_form(grown.conj().T).T / (NX * NY)
    as32 = lambda x: np.asarray(x, np.float32)
    return {
        "row_first": as32(np.stack(row_first)),
        "row_twist": as32(np.stack(row_twist)),
        "outer": as32(outer),
        "col_twist": as32(col_twist),
        "col_small": as32(np.stack([col_small, col_back])),
        "back_twist": as32(np.stack(back_twist)),
        "back_last": as32(np.stack(back_last)),
    }


TABLES = make_tables()


def dot(left, right):
    return lax.dot_general(
        left, right, (((1,), (0,)), ((), ())), precision=highest, preferred_element_type=jnp.float32
    )


def dot_t(left, right):
    return lax.dot_general(
        left, right, (((1,), (1,)), ((), ())), precision=highest, preferred_element_type=jnp.float32
    )


def tiles_of(cells):
    return jnp.concatenate([cells[:, LANES * n : LANES * (n + 1)] for n in range(SUBS)], 0)


def swap_halves(x, sign):
    return pltpu.roll(x, 64, 1) * sign


def half_sign(first, second):
    lane = lax.broadcasted_iota(jnp.int32, (LANES, LANES), 1)
    return jnp.where(lane < 64, jnp.float32(first), jnp.float32(second))


def quarter_turn(k, direction):
    k = k % 4
    real = jnp.where(k == 0, 1.0, jnp.where(k == 2, -1.0, 0.0)).astype(jnp.float32)
    imag = jnp.where(k == 1, direction, jnp.where(k == 3, -direction, 0.0)).astype(jnp.float32)
    return real, imag


def parity_sign(q):
    return jnp.where(q % 2 == 0, 1.0, -1.0).astype(jnp.float32)


def row_spectra(q, blocks, first, twist, outer):
    sign = parity_sign(q)
    own_real, own_imag = quarter_turn(q * q, -1.0)
    mate_real, mate_imag = quarter_turn((q ^ 1) * q, -1.0)
    powers = []
    for real, imag, height in blocks:
        levels = [(real, imag)]
        for _ in range(2):
            levels.append((levels[-1][0] * height, levels[-1][1] * height))
        powers.append(levels)
    stacked = []
    for b in range(3):
        same = [powers[0][b][k] + sign * powers[1][b][k] for k in range(2)]
        mate = [powers[2][b][k] + sign * powers[3][b][k] for k in range(2)]
        merged_real = (own_real * same[0] - own_imag * same[1]) + (
            mate_real * mate[0] - mate_imag * mate[1]
        )
        merged_imag = (own_real * same[1] + own_imag * same[0]) + (
            mate_real * mate[1] + mate_imag * mate[0]
        )
        stacked.append(jnp.concatenate([merged_real, merged_imag], 0))
    stepped = dot(first, jnp.concatenate(stacked, 1))
    turned = []
    for b in range(3):
        part = stepped[:, LANES * b : LANES * (b + 1)]
        real, imag = part[:HALF], part[HALF:]
        z_real = real * twist[0] - imag * twist[1]
        z_imag = real * twist[1] + imag * twist[0]
        turned.append(
            jnp.concatenate(
                [
                    jnp.concatenate([z_real, z_imag], 1),
                    jnp.concatenate([z_imag, -z_real], 1),
                ],
                0,
            )
        )
    return dot_t(outer, jnp.concatenate(turned, 0))


def column_stage(blocks, kernels, outer, twist, small, small_back):
    plus_minus = half_sign(1.0, -1.0)
    minus_plus = half_sign(-1.0, 1.0)
    lower = [swap_halves(x, plus_minus) for x in blocks]
    stepped = dot(
        outer, jnp.concatenate([jnp.concatenate(blocks, 1), jnp.concatenate(lower, 1)], 0)
    )
    turned = []
    for b in range(3):
        part = stepped[:, LANES * b : LANES * (b + 1)]
        turned.append(part * twist[0] + pltpu.roll(part, 64, 1) * twist[1])
    spectra = dot(jnp.concatenate(turned, 0), small)
    plain = [spectra[LANES * b : LANES * (b + 1)] for b in range(3)]
    rolled = [pltpu.roll(x, 64, 1) for x in plain]

    def times(m, b):
        return kernels[m][0] * plain[b] + kernels[m][1] * rolled[b]

    mixed = [
        times(0, 0) - times(1, 1) + times(2, 2),
        times(1, 0) - 2.0 * times(2, 1),
        times(2, 0),
    ]
    back = dot(jnp.concatenate(mixed, 0), small_back)
    upper, under = [], []
    for a in range(3):
        part = back[LANES * a : LANES * (a + 1)]
        turned = part * twist[0] - pltpu.roll(part, 64, 1) * twist[1]
        upper.append(turned)
        under.append(swap_halves(turned, minus_plus))
    return dot(outer, jnp.concatenate([jnp.concatenate(upper, 1), jnp.concatenate(under, 1)], 0))


def row_inverse(q, blocks, heights, outer, twist, last):
    minus_plus = half_sign(-1.0, 1.0)
    under = [swap_halves(x, minus_plus) for x in blocks]
    stepped = dot(
        outer, jnp.concatenate([jnp.concatenate(blocks, 1), jnp.concatenate(under, 1)], 0)
    )
    turned = []
    for a in range(3):
        part = stepped[:, LANES * a : LANES * (a + 1)]
        turned.append(part * twist[0] + pltpu.roll(part, 64, 1) * twist[1])
    fields = dot_t(last, jnp.concatenate(turned, 0))
    level = [fields[:, LANES * a : LANES * (a + 1)] for a in range(3)]
    sums = []
    for m, height in zip((0, 2, 1, 3), heights):
        scale_real, scale_imag = quarter_turn((q ^ m) * q, 1.0)
        real = (level[2][:HALF] * height + level[1][:HALF]) * height + level[0][:HALF]
        imag = (level[2][HALF:] * height + level[1][HALF:]) * height + level[0][HALF:]
        sums.append((scale_real * real - scale_imag * imag, scale_real * imag + scale_imag * real))
    return sums


vmem = pl.BlockSpec(memory_space=pltpu.VMEM)


def call(body, shapes, *args, loose=0, scratch=(), flops=1_000_000, moved=1_000_000):
    specs = [vmem] * (len(args) - loose) + [pl.BlockSpec(memory_space=pl.ANY)] * loose
    return pl.pallas_call(
        body,
        out_shape=shapes,
        in_specs=specs,
        out_specs=jax.tree.map(lambda _: vmem, shapes),
        scratch_shapes=scratch,
        compiler_params=pltpu.CompilerParams(vmem_limit_bytes=40 * 1024 * 1024),
        cost_estimate=pl.CostEstimate(flops=flops, bytes_accessed=moved, transcendentals=0),
    )(*args)


def f32(*shape):
    return jax.ShapeDtypeStruct(shape, jnp.float32)


def row_kernel(own_ref, far_ref, mate_ref, diag_ref, first_ref, twist_ref, outer_ref, out_ref):
    q = lax.axis_index("gy")
    blocks = [
        [tiles_of(ref[part]) for part in range(3)] for ref in (own_ref, far_ref, mate_ref, diag_ref)
    ]
    out = row_spectra(q, blocks, first_ref[q], twist_ref[q], outer_ref[...])
    for b in range(3):
        out_ref[pl.ds(b, DEV_X, stride=3), :] = out[:, LANES * b : LANES * (b + 1)]


def table_kernel(flat_ref, slope_ref, curve_ref, out_ref):
    lane = lax.broadcasted_iota(jnp.int32, (64, LANES), 1)
    for m, ref in enumerate((flat_ref, slope_ref, curve_ref)):
        real = ref[pl.ds(0, 64, stride=2), :]
        imag = ref[pl.ds(1, 64, stride=2), :]
        for parity in range(2):
            low = lane < 64 if parity == 0 else lane >= 64
            both_real = jnp.where(low, real, pltpu.roll(real, 64, 1))
            both_imag = jnp.where(low, imag, pltpu.roll(imag, 64, 1))
            out_ref[2 * m, pl.ds(parity, 64, stride=2), :] = both_real
            out_ref[2 * m + 1, pl.ds(parity, 64, stride=2), :] = jnp.where(
                lane < 64, -both_imag, both_imag
            )


def column_kernel(in_ref, table_ref, outer_ref, twist_ref, small_ref, after_ref, out_ref):
    blocks = [in_ref[pl.ds(b, DEV_X, stride=3), :] for b in range(3)]
    kernels = [(table_ref[2 * m], table_ref[2 * m + 1]) for m in range(3)]
    out = column_stage(blocks, kernels, outer_ref[...], twist_ref, small_ref[0], small_ref[1])
    for a in range(3):
        out_ref[pl.ds(a, DEV_X, stride=3), :] = out[:, LANES * a : LANES * (a + 1)]


def inverse_kernel(
    in_ref,
    own_ref,
    far_ref,
    mate_ref,
    diag_ref,
    outer_ref,
    twist_ref,
    last_ref,
    after_ref,
    same_ref,
    mate_out_ref,
):
    q = lax.axis_index("gy")
    blocks = [in_ref[pl.ds(a, DEV_X, stride=3), :] for a in range(3)]
    heights = [tiles_of(ref[2]) for ref in (own_ref, far_ref, mate_ref, diag_ref)]
    sums = row_inverse(q, blocks, heights, outer_ref[...], twist_ref[q], last_ref[q])
    places = ((same_ref, 0), (same_ref, 1), (mate_out_ref, 0), (mate_out_ref, 1))
    for (ref, slot), pair in zip(places, sums):
        for part in range(2):
            for n in range(SUBS):
                ref[slot, part, :, LANES * n : LANES * (n + 1)] = pair[part][
                    ROWS * n : ROWS * (n + 1)
                ]


X_TOP = 1.31


def fit(function, degree):
    cheb = np.polynomial.chebyshev.Chebyshev.interpolate(function, degree, [0.0, X_TOP])
    power = cheb.convert(kind=np.polynomial.Polynomial, domain=[-1, 1], window=[-1, 1])
    moved = power(np.polynomial.Polynomial([X_TOP / 2, 1.0]))
    return [float(c) for c in moved.coef[::-1]]


COS_FIT = fit(lambda x: np.cos(wave_number * np.sqrt(x)), 10)
SIN_FIT = fit(
    lambda x: wave_number * np.sinc(2.0 * np.sqrt(x)),
    9,
)


def near_table(kinds):
    cell = np.arange(TILE)
    entries = []
    for shift_row, shift_col in kinds:
        for sr in range(TILE):
            for sc in range(TILE):
                dr = (cell + sr) % TILE - cell + TILE * shift_row
                dc = (cell + sc) % TILE - cell + TILE * shift_col
                rho2 = spacing * spacing * (dr[:, None] ** 2 + dc[None, :] ** 2)
                radius = np.sqrt(rho2 + lift_height**2)
                green = np.exp(1j * wave_number * radius) / radius
                log_slope = 1j * wave_number - 1 / radius
                first_r = green * log_slope
                second_r = green * (log_slope**2 + 1 / radius**2)
                rise = lift_height / radius
                k1 = first_r * rise
                k2 = 0.5 * (second_r * rise**2 + first_r * (1 - rise**2) / radius)
                a0 = green - lift_height * k1 + lift_height**2 * k2
                a1 = k1 - 2 * lift_height * k2
                entry = [rho2, a0.real, a1.real, k2.real, a0.imag, a1.imag, k2.imag]
                entries.append([np.tile(e, (ROWS // TILE, LANES // TILE)) for e in entry])
    return np.asarray(entries, np.float32)


SIDE_KINDS = ((0, 0), (0, -1), (0, 1))
OVER_KINDS = ((-1, 0), (1, 0))
SIDE_TABLE = near_table(SIDE_KINDS)
OVER_TABLE = near_table(OVER_KINDS)


def horner(coefficients, x):
    total = coefficients[0] * x + coefficients[1]
    for c in coefficients[2:]:
        total = total * x + c
    return total


def turned_index(axis, turn):
    place = lax.broadcasted_iota(jnp.int32, (ROWS, LANES), axis)
    within = place % TILE
    return place - within + (within + turn) % TILE


def turn_cells(x, axis, turn):
    if turn == 0:
        return x
    return jnp.take_along_axis(x, turned_index(axis, turn), axis=axis)


def meet(raised, source, table_ref, entry):
    real, imag, height = source
    w = raised - height
    v = w * w
    x = v + table_ref[entry, 0]
    u = x - X_TOP / 2
    root = lax.rsqrt(x)
    gap_real = horner(COS_FIT, u) * root - (
        table_ref[entry, 2] * w + (table_ref[entry, 3] * v + table_ref[entry, 1])
    )
    gap_imag = horner(SIN_FIT, u) - (
        table_ref[entry, 5] * w + (table_ref[entry, 6] * v + table_ref[entry, 4])
    )
    return gap_real * real - gap_imag * imag, gap_real * imag + gap_imag * real


def meet_tiles(raised, sources, table_ref):
    total_real = jnp.zeros((ROWS, LANES), jnp.float32)
    total_imag = jnp.zeros((ROWS, LANES), jnp.float32)
    for kind, source in enumerate(sources):
        for sc in range(TILE):
            column = [turn_cells(x, 1, sc) for x in source]
            for sr in range(TILE):
                cells = [turn_cells(x, 0, sr) for x in column]
                entry = (kind * TILE + sr) * TILE + sc
                real, imag = meet(raised, cells, table_ref, entry)
                total_real = total_real + real
                total_imag = total_imag + imag
    return total_real, total_imag


def side_kernel(own_ref, far_ref, mate_ref, diag_ref, table_ref, after_ref, out_ref, rows_ref, edge):
    q = lax.axis_index("gy")
    odd = q % 2 == 1
    for part in range(3):
        last = slice(SPAN - LANES, SPAN)
        first = slice(0, LANES)
        edge[0, part] = jnp.where(odd, mate_ref[part, :, last], diag_ref[part, :, last])
        edge[SUBS + 1, part] = jnp.where(odd, diag_ref[part, :, first], mate_ref[part, :, first])
        for n in range(SUBS):
            edge[n + 1, part] = own_ref[part, :, LANES * n : LANES * (n + 1)]
    rows_ref[...] = own_ref[...]
    lane = lax.broadcasted_iota(jnp.int32, (ROWS, LANES), 1)

    for n in range(SUBS):
        before = [edge[n, part] for part in range(3)]
        here = [edge[n + 1, part] for part in range(3)]
        after = [edge[n + 2, part] for part in range(3)]
        left = [
            jnp.where(lane < TILE, pltpu.roll(x, TILE, 1), pltpu.roll(y, TILE, 1))
            for x, y in zip(before, here)
        ]
        right = [
            jnp.where(
                lane < LANES - TILE,
                pltpu.roll(y, LANES - TILE, 1),
                pltpu.roll(z, LANES - TILE, 1),
            )
            for y, z in zip(here, after)
        ]
        real, imag = meet_tiles(here[2] + lift_height, (here, left, right), table_ref)
        out_ref[0, :, LANES * n : LANES * (n + 1)] = area_weight * real
        out_ref[1, :, LANES * n : LANES * (n + 1)] = area_weight * imag


def over_kernel(own_ref, up_ref, down_ref, table_ref, side_ref, after_ref, out_ref):
    sub = lax.broadcasted_iota(jnp.int32, (ROWS, LANES), 0)
    for n in range(SUBS):
        lanes = slice(LANES * n, LANES * (n + 1))
        here = [own_ref[part, :, lanes] for part in range(3)]
        swapped = [pltpu.roll(x, TILE, 0) for x in here]
        above = [
            jnp.where(sub < TILE, pltpu.roll(up_ref[part, :, lanes], TILE, 0), swapped[part])
            for part in range(3)
        ]
        below = [
            jnp.where(sub < TILE, swapped[part], pltpu.roll(down_ref[part, :, lanes], TILE, 0))
            for part in range(3)
        ]
        real, imag = meet_tiles(here[2] + lift_height, (above, below), table_ref)
        out_ref[0, :, lanes] = side_ref[0, :, lanes] + area_weight * real
        out_ref[1, :, lanes] = side_ref[1, :, lanes] + area_weight * imag


def all_to_all_x(messages):
    shaped = messages.reshape(DEV_X, 1, 3 * LANES)
    moved = lax.all_to_all(shaped, "gx", split_axis=0, concat_axis=0, tiled=True)
    return moved.reshape(3 * DEV_X, LANES)


def local(unknown, height, spectrum_flat, spectrum_slope, spectrum_curve):
    mate_pairs = [(g, g ^ 1) for g in range(DEV_Y)]
    far_pairs = [(g, g ^ 2) for g in range(DEV_Y)]
    own = jnp.concatenate([unknown, height[None]], 0)
    far = lax.ppermute(own, "gy", far_pairs)
    mate = lax.ppermute(own, "gy", mate_pairs)
    diagonal = lax.ppermute(far, "gy", mate_pairs)
    groups = (own, far, mate, diagonal)

    lined = [
        s.reshape(2, 64, LANES).transpose(1, 0, 2).reshape(2 * 64, LANES)
        for s in (spectrum_flat, spectrum_slope, spectrum_curve)
    ]
    table = call(table_kernel, f32(6, LANES, LANES), *lined)

    sent = call(
        row_kernel,
        f32(3 * DEV_X, LANES),
        *groups,
        TABLES["row_first"],
        TABLES["row_twist"],
        TABLES["outer"],
    )
    arrived = all_to_all_x(sent)
    side, rows = call(
        side_kernel,
        (f32(2, ROWS, SPAN), f32(3, ROWS, SPAN)),
        *groups,
        SIDE_TABLE,
        sent,
        loose=1,
        scratch=[pltpu.VMEM((SUBS + 2, 3, ROWS, LANES), jnp.float32)],
        flops=30_000_000,
    )
    up = lax.ppermute(rows, "gx", [(i, (i + 1) % DEV_X) for i in range(DEV_X)])
    down = lax.ppermute(rows, "gx", [((i + 1) % DEV_X, i) for i in range(DEV_X)])
    back = call(
        column_kernel,
        f32(3 * DEV_X, LANES),
        arrived,
        table,
        TABLES["outer"],
        TABLES["col_twist"],
        TABLES["col_small"],
        side,
        loose=1,
    )
    returned = all_to_all_x(back)
    near = call(
        over_kernel,
        f32(2, ROWS, SPAN),
        own,
        up,
        down,
        OVER_TABLE,
        side,
        back,
        loose=1,
        flops=20_000_000,
    )
    same, crossed = call(
        inverse_kernel,
        (f32(2, 2, ROWS, SPAN), f32(2, 2, ROWS, SPAN)),
        returned,
        *groups,
        TABLES["outer"],
        TABLES["back_twist"],
        TABLES["back_last"],
        near,
        loose=1,
    )
    from_mate = lax.ppermute(crossed, "gy", mate_pairs)
    from_far = lax.ppermute(same[1] + from_mate[1], "gy", far_pairs)
    return (same[0] + from_mate[0] + near) + from_far


def solution(mesh):
    return jax.shard_map(
        local,
        mesh=mesh,
        in_specs=(
            P(None, "gx", "gy"),
            P("gx", "gy"),
            P(None, ("gx", "gy")),
            P(None, ("gx", "gy")),
            P(None, ("gx", "gy")),
        ),
        out_specs=P(None, "gx", "gy"),
        check_vma=False,
    )
```

```python
import functools
import math

import jax
import jax.numpy as jnp
import ml_dtypes
import numpy as np
from jax import lax
from jax.experimental import pallas as pl
from jax.experimental.pallas import tpu as pltpu
from jax.sharding import PartitionSpec as P

TILE = 4
wave_number = 2.0 * math.pi
spacing = 0.1
lift_height = 0.05
area_weight = spacing * spacing

ROWS = 8
SPAN = 1024
DEV_X = 128
DEV_Y = 4
LANES = 128
SUBS = SPAN // LANES
NARROW = 8
NX = ROWS * DEV_X
NY = SPAN * DEV_Y
HALF = ROWS * NARROW


def real_form(coeff):
    return np.block([[coeff.real, -coeff.imag], [coeff.imag, coeff.real]])


def halves(matrix):
    high = matrix.astype(ml_dtypes.bfloat16).astype(np.float64)
    low = (matrix - high).astype(ml_dtypes.bfloat16).astype(np.float64)
    return np.stack([high, low]).astype(np.float32)


def make_tables():
    r8 = np.arange(8)
    lane = np.arange(LANES)
    eye = np.eye(8)
    row_first, row_twist, back_twist, back_last = [], [], [], []
    for q in range(DEV_Y):
        small = np.exp(-2j * np.pi * (np.outer(r8, r8) / 8 + r8[None, :] * q / 32))
        grown = np.einsum("cn,rs->rcns", small, eye).reshape(HALF, HALF)
        row_first.append(real_form(grown))
        phase = np.exp(-2j * np.pi * lane[None, :] * (r8[:, None] / 1024 + q / 4096))
        phase = np.tile(phase, (8, 1))
        row_twist.append(np.stack([phase.real, phase.imag]))
        turn = phase.conj().T
        back_twist.append(
            np.stack(
                [
                    np.concatenate([turn.real, turn.real], 1),
                    np.concatenate([-turn.imag, turn.imag], 1),
                ]
            )
        )
        wide = np.einsum("cn,rs->nrsc", small.conj(), eye).reshape(HALF, HALF)
        back_last.append(real_form(wide))
    ring = 2 * np.pi * np.outer(lane, lane) / LANES
    outer = np.concatenate([np.cos(ring), np.sin(ring)], 1)
    turn = np.exp(-2j * np.pi * np.outer(lane, np.repeat(r8, NARROW)) / NX)
    col_twist = np.stack(
        [
            np.concatenate([turn.real, turn.real], 1),
            np.concatenate([-turn.imag, turn.imag], 1),
        ]
    )
    ring8 = np.exp(-2j * np.pi * np.outer(r8, r8) / 8)
    grown = np.kron(ring8, np.eye(NARROW))
    col_small = real_form(grown).T
    col_back = real_form(grown.conj().T).T / (NX * NY)
    as32 = lambda x: np.asarray(x, np.float32)
    return {
        "row_first": np.stack([halves(x) for x in row_first]),
        "row_twist": as32(np.stack(row_twist)),
        "outer": halves(outer),
        "col_twist": as32(col_twist),
        "col_small": np.stack([halves(col_small), halves(col_back)]),
        "back_twist": as32(np.stack(back_twist)),
        "back_last": np.stack([halves(x) for x in back_last]),
    }


TABLES = make_tables()


def parts_of(x):
    high = x.astype(jnp.bfloat16)
    return high, (x - high.astype(jnp.float32)).astype(jnp.bfloat16)


def product(left, right, dims):
    def one(x, y):
        return lax.dot_general(x, y, (dims, ((), ())), preferred_element_type=jnp.float32)

    return one(left[0], right[0]) + (one(left[0], right[1]) + one(left[1], right[0]))


def dot(left, right):
    return product(left, right, ((1,), (0,)))


def dot_t(left, right):
    return product(left, right, ((1,), (1,)))


def table_parts(ref):
    return ref[0].astype(jnp.bfloat16), ref[1].astype(jnp.bfloat16)


def tiles_of(cells):
    return jnp.concatenate([cells[:, LANES * n : LANES * (n + 1)] for n in range(SUBS)], 0)


def swap_halves(x, sign):
    return pltpu.roll(x, 64, 1) * sign


def half_sign(first, second):
    lane = lax.broadcasted_iota(jnp.int32, (LANES, LANES), 1)
    return jnp.where(lane < 64, jnp.float32(first), jnp.float32(second))


def quarter_turn(k, direction):
    k = k % 4
    real = jnp.where(k == 0, 1.0, jnp.where(k == 2, -1.0, 0.0)).astype(jnp.float32)
    imag = jnp.where(k == 1, direction, jnp.where(k == 3, -direction, 0.0)).astype(jnp.float32)
    return real, imag


def parity_sign(q):
    return jnp.where(q % 2 == 0, 1.0, -1.0).astype(jnp.float32)


def row_spectra(q, blocks, first, twist, outer):
    sign = parity_sign(q)
    own_real, own_imag = quarter_turn(q * q, -1.0)
    mate_real, mate_imag = quarter_turn((q ^ 1) * q, -1.0)
    powers = []
    for real, imag, height in blocks:
        levels = [(real, imag)]
        for _ in range(2):
            levels.append((levels[-1][0] * height, levels[-1][1] * height))
        powers.append(levels)
    stacked = []
    for b in range(3):
        same = [powers[0][b][k] + sign * powers[1][b][k] for k in range(2)]
        mate = [powers[2][b][k] + sign * powers[3][b][k] for k in range(2)]
        merged_real = (own_real * same[0] - own_imag * same[1]) + (
            mate_real * mate[0] - mate_imag * mate[1]
        )
        merged_imag = (own_real * same[1] + own_imag * same[0]) + (
            mate_real * mate[1] + mate_imag * mate[0]
        )
        stacked.append(jnp.concatenate([merged_real, merged_imag], 0))
    stepped = dot(first, parts_of(jnp.concatenate(stacked, 1)))
    turned = []
    for b in range(3):
        part = stepped[:, LANES * b : LANES * (b + 1)]
        real, imag = part[:HALF], part[HALF:]
        z_real = real * twist[0] - imag * twist[1]
        z_imag = real * twist[1] + imag * twist[0]
        turned.append(
            jnp.concatenate(
                [
                    jnp.concatenate([z_real, z_imag], 1),
                    jnp.concatenate([z_imag, -z_real], 1),
                ],
                0,
            )
        )
    return dot_t(outer, parts_of(jnp.concatenate(turned, 0)))


def column_stage(blocks, kernels, outer, twist, small, small_back):
    plus_minus = half_sign(1.0, -1.0)
    minus_plus = half_sign(-1.0, 1.0)
    lower = [swap_halves(x, plus_minus) for x in blocks]
    stepped = dot(
        outer,
        parts_of(jnp.concatenate([jnp.concatenate(blocks, 1), jnp.concatenate(lower, 1)], 0)),
    )
    turned = []
    for b in range(3):
        part = stepped[:, LANES * b : LANES * (b + 1)]
        turned.append(part * twist[0] + pltpu.roll(part, 64, 1) * twist[1])
    spectra = dot(parts_of(jnp.concatenate(turned, 0)), small)
    plain = [spectra[LANES * b : LANES * (b + 1)] for b in range(3)]
    rolled = [pltpu.roll(x, 64, 1) for x in plain]

    def times(m, b):
        return kernels[m][0] * plain[b] + kernels[m][1] * rolled[b]

    mixed = [
        times(0, 0) - times(1, 1) + times(2, 2),
        times(1, 0) - 2.0 * times(2, 1),
        times(2, 0),
    ]
    back = dot(parts_of(jnp.concatenate(mixed, 0)), small_back)
    upper, under = [], []
    for a in range(3):
        part = back[LANES * a : LANES * (a + 1)]
        turned = part * twist[0] - pltpu.roll(part, 64, 1) * twist[1]
        upper.append(turned)
        under.append(swap_halves(turned, minus_plus))
    return dot(
        outer, parts_of(jnp.concatenate([jnp.concatenate(upper, 1), jnp.concatenate(under, 1)], 0))
    )


def row_inverse(q, blocks, heights, outer, twist, last):
    minus_plus = half_sign(-1.0, 1.0)
    under = [swap_halves(x, minus_plus) for x in blocks]
    stepped = dot(
        outer,
        parts_of(jnp.concatenate([jnp.concatenate(blocks, 1), jnp.concatenate(under, 1)], 0)),
    )
    turned = []
    for a in range(3):
        part = stepped[:, LANES * a : LANES * (a + 1)]
        turned.append(part * twist[0] + pltpu.roll(part, 64, 1) * twist[1])
    fields = dot_t(last, parts_of(jnp.concatenate(turned, 0)))
    level = [fields[:, LANES * a : LANES * (a + 1)] for a in range(3)]
    sums = []
    for m, height in zip((0, 2, 1, 3), heights):
        scale_real, scale_imag = quarter_turn((q ^ m) * q, 1.0)
        real = (level[2][:HALF] * height + level[1][:HALF]) * height + level[0][:HALF]
        imag = (level[2][HALF:] * height + level[1][HALF:]) * height + level[0][HALF:]
        sums.append((scale_real * real - scale_imag * imag, scale_real * imag + scale_imag * real))
    return sums


vmem = pl.BlockSpec(memory_space=pltpu.VMEM)


def call(body, shapes, *args, loose=0, waits=0, scratch=(), flops=1_000_000, moved=1_000_000):
    blocks = len(args) - loose - waits
    specs = [vmem] * blocks + [pl.BlockSpec(memory_space=pl.ANY)] * (loose + waits)
    kept = list(args)
    for n in range(blocks, blocks + loose):
        kept[n] = pltpu.with_memory_space_constraint(jnp.asarray(args[n]), pltpu.HBM)
    return pl.pallas_call(
        body,
        out_shape=shapes,
        in_specs=specs,
        out_specs=jax.tree.map(lambda _: vmem, shapes),
        scratch_shapes=scratch,
        compiler_params=pltpu.CompilerParams(vmem_limit_bytes=40 * 1024 * 1024),
        cost_estimate=pl.CostEstimate(flops=flops, bytes_accessed=moved, transcendentals=0),
    )(*kept)


def held(*shape):
    return pltpu.VMEM(shape, jnp.float32)


def f32(*shape):
    return jax.ShapeDtypeStruct(shape, jnp.float32)


def fetch(pairs, sems):
    copies = [pltpu.make_async_copy(src, dst, sems.at[n]) for n, (src, dst) in enumerate(pairs)]
    for copy in copies:
        copy.start()
    return copies


def pack_kernel(
    unknown_ref, height_ref, first_ref, twist_ref, outer_ref, own_ref, first_out, twist_out, outer_out, sems
):
    q = lax.axis_index("gy")
    copies = fetch(
        [
            (unknown_ref, own_ref.at[pl.ds(0, 2)]),
            (height_ref, own_ref.at[2]),
            (first_ref.at[q], first_out),
            (twist_ref.at[q], twist_out),
            (outer_ref, outer_out),
        ],
        sems,
    )
    for copy in copies:
        copy.wait()


def row_kernel(
    own_ref, far_ref, mate_ref, diag_ref, first_ref, twist_ref, outer_ref, out_ref, low_ref
):
    q = lax.axis_index("gy")
    blocks = [
        [tiles_of(ref[part]) for part in range(3)] for ref in (own_ref, far_ref, mate_ref, diag_ref)
    ]
    out = row_spectra(q, blocks, table_parts(first_ref), twist_ref, table_parts(outer_ref))
    for b in range(3):
        out_ref[pl.ds(b, DEV_X, stride=3), :] = out[:, LANES * b : LANES * (b + 1)]
    low_ref[...] = own_ref[:, TILE:]


def spread_spectra(refs, out_ref):
    lane = lax.broadcasted_iota(jnp.int32, (64, LANES), 1)
    for m, ref in enumerate(refs):
        real = ref[pl.ds(0, 64, stride=2), :]
        imag = ref[pl.ds(1, 64, stride=2), :]
        for parity in range(2):
            low = lane < 64 if parity == 0 else lane >= 64
            both_real = jnp.where(low, real, pltpu.roll(real, 64, 1))
            both_imag = jnp.where(low, imag, pltpu.roll(imag, 64, 1))
            out_ref[2 * m, pl.ds(parity, 64, stride=2), :] = both_real
            out_ref[2 * m + 1, pl.ds(parity, 64, stride=2), :] = jnp.where(
                lane < 64, -both_imag, both_imag
            )


def column_kernel(
    in_ref, spread_ref, outer_ref, twist_ref, small_ref, own_ref, after_ref, out_ref, high_ref
):
    blocks = [in_ref[pl.ds(b, DEV_X, stride=3), :] for b in range(3)]
    kernels = [(spread_ref[2 * m], spread_ref[2 * m + 1]) for m in range(3)]
    out = column_stage(
        blocks,
        kernels,
        table_parts(outer_ref),
        twist_ref,
        table_parts(small_ref.at[0]),
        table_parts(small_ref.at[1]),
    )
    for a in range(3):
        out_ref[pl.ds(a, DEV_X, stride=3), :] = out[:, LANES * a : LANES * (a + 1)]
    high_ref[...] = own_ref[:, :TILE]


def inverse_kernel(
    in_ref,
    own_ref,
    far_ref,
    mate_ref,
    diag_ref,
    outer_ref,
    twist_ref,
    last_ref,
    down_ref,
    same_ref,
    crossed_ref,
):
    q = lax.axis_index("gy")
    blocks = [in_ref[pl.ds(a, DEV_X, stride=3), :] for a in range(3)]
    heights = [tiles_of(ref[2]) for ref in (own_ref, far_ref, mate_ref, diag_ref)]
    sums = row_inverse(
        q, blocks, heights, table_parts(outer_ref), twist_ref, table_parts(last_ref)
    )
    places = ((same_ref, 0), (same_ref, 1), (crossed_ref, 0), (crossed_ref, 1))
    for (ref, slot), pair in zip(places, sums):
        for part in range(2):
            for n in range(SUBS):
                ref[slot, part, :, LANES * n : LANES * (n + 1)] = pair[part][
                    ROWS * n : ROWS * (n + 1)
                ]


X_TOP = 1.31


def fit(function, degree):
    cheb = np.polynomial.chebyshev.Chebyshev.interpolate(function, degree, [0.0, X_TOP])
    power = cheb.convert(kind=np.polynomial.Polynomial, domain=[-1, 1], window=[-1, 1])
    moved = power(np.polynomial.Polynomial([X_TOP / 2, 1.0]))
    return [float(c) for c in moved.coef[::-1]]


COS_FIT = fit(lambda x: np.cos(wave_number * np.sqrt(x)), 9)
SIN_FIT = fit(lambda x: wave_number * np.sinc(2.0 * np.sqrt(x)), 8)


def near_table(kinds):
    cell = np.arange(TILE)
    entries = []
    for shift_row, shift_col in kinds:
        for sr in range(TILE):
            for sc in range(TILE):
                dr = (cell + sr) % TILE - cell + TILE * shift_row
                dc = (cell + sc) % TILE - cell + TILE * shift_col
                rho2 = spacing * spacing * (dr[:, None] ** 2 + dc[None, :] ** 2)
                radius = np.sqrt(rho2 + lift_height**2)
                green = np.exp(1j * wave_number * radius) / radius
                log_slope = 1j * wave_number - 1 / radius
                first_r = green * log_slope
                second_r = green * (log_slope**2 + 1 / radius**2)
                rise = lift_height / radius
                k1 = first_r * rise
                k2 = 0.5 * (second_r * rise**2 + first_r * (1 - rise**2) / radius)
                a0 = green - lift_height * k1 + lift_height**2 * k2
                a1 = k1 - 2 * lift_height * k2
                offset = rho2 - X_TOP / 2
                line = SIN_FIT[-2] - k2.imag
                level = SIN_FIT[-1] - a0.imag + k2.imag * offset
                entry = [offset, a0.real, a1.real, k2.real, level, line, a1.imag]
                entries.append([np.tile(e, (ROWS // TILE, LANES // TILE)) for e in entry])
    return np.asarray(entries, np.float32)


SIDE_KINDS = ((0, 0), (0, -1), (0, 1))
OVER_KINDS = ((-1, 0), (1, 0))
SIDE_TABLE = near_table(SIDE_KINDS)
OVER_TABLE = near_table(OVER_KINDS)


def horner(coefficients, x):
    total = coefficients[0] * x + coefficients[1]
    for c in coefficients[2:]:
        total = total * x + c
    return total


def turned_index(axis, turn):
    place = lax.broadcasted_iota(jnp.int32, (ROWS, LANES), axis)
    within = place % TILE
    return place - within + (within + turn) % TILE


def turn_cells(x, axis, turn):
    if turn == 0:
        return x
    return jnp.take_along_axis(x, turned_index(axis, turn), axis=axis)


def meet(raised, source, table_ref, entry):
    real, imag, height = source
    w = raised - height
    v = w * w
    u = v + table_ref[entry, 0]
    root = lax.rsqrt(u + X_TOP / 2)
    gap_real = horner(COS_FIT, u) * root - (
        table_ref[entry, 2] * w + (table_ref[entry, 3] * v + table_ref[entry, 1])
    )
    fitted = (horner(SIN_FIT[:-2], u) * u + table_ref[entry, 5]) * u + table_ref[entry, 4]
    gap_imag = fitted - table_ref[entry, 6] * w
    return gap_real * real - gap_imag * imag, gap_real * imag + gap_imag * real


def meet_tiles(raised, sources, table_ref):
    total_real = jnp.zeros((ROWS, LANES), jnp.float32)
    total_imag = jnp.zeros((ROWS, LANES), jnp.float32)
    for kind, source in enumerate(sources):
        for sc in range(TILE):
            column = [turn_cells(x, 1, sc) for x in source]
            for sr in range(TILE):
                cells = [turn_cells(x, 0, sr) for x in column]
                entry = (kind * TILE + sr) * TILE + sc
                real, imag = meet(raised, cells, table_ref, entry)
                total_real = total_real + real
                total_imag = total_imag + imag
    return total_real, total_imag


def spread_kernel(
    flat_ref,
    slope_ref,
    curve_ref,
    twist_ref,
    small_ref,
    after_ref,
    spread_ref,
    twist_out,
    small_out,
    lined,
    sems,
):
    copies = fetch(
        [
            (flat_ref, lined.at[0]),
            (slope_ref, lined.at[1]),
            (curve_ref, lined.at[2]),
            (twist_ref, twist_out),
            (small_ref, small_out),
        ],
        sems,
    )
    for copy in copies:
        copy.wait()
    spread_spectra([lined.at[m] for m in range(3)], spread_ref)


def side_kernel(
    own_ref,
    far_ref,
    mate_ref,
    diag_ref,
    table_ref,
    back_twist_ref,
    back_last_ref,
    after_ref,
    out_ref,
    back_twist_out,
    back_last_out,
    edge,
    sems,
):
    q = lax.axis_index("gy")
    copies = fetch(
        [(back_twist_ref.at[q], back_twist_out), (back_last_ref.at[q], back_last_out)], sems
    )
    odd = q % 2 == 1
    for part in range(3):
        last = slice(SPAN - LANES, SPAN)
        first = slice(0, LANES)
        edge[0, part] = jnp.where(odd, mate_ref[part, :, last], diag_ref[part, :, last])
        edge[SUBS + 1, part] = jnp.where(odd, diag_ref[part, :, first], mate_ref[part, :, first])
        for n in range(SUBS):
            edge[n + 1, part] = own_ref[part, :, LANES * n : LANES * (n + 1)]
    lane = lax.broadcasted_iota(jnp.int32, (ROWS, LANES), 1)

    for n in range(SUBS):
        before = [edge[n, part] for part in range(3)]
        here = [edge[n + 1, part] for part in range(3)]
        after = [edge[n + 2, part] for part in range(3)]
        left = [
            jnp.where(lane < TILE, pltpu.roll(x, TILE, 1), pltpu.roll(y, TILE, 1))
            for x, y in zip(before, here)
        ]
        right = [
            jnp.where(
                lane < LANES - TILE,
                pltpu.roll(y, LANES - TILE, 1),
                pltpu.roll(z, LANES - TILE, 1),
            )
            for y, z in zip(here, after)
        ]
        real, imag = meet_tiles(here[2] + lift_height, (here, left, right), table_ref)
        out_ref[0, :, LANES * n : LANES * (n + 1)] = area_weight * real
        out_ref[1, :, LANES * n : LANES * (n + 1)] = area_weight * imag
    for copy in copies:
        copy.wait()


def over_kernel(own_ref, up_ref, down_ref, table_ref, side_ref, same_ref, mate_ref, out_ref):
    for n in range(SUBS):
        lanes = slice(LANES * n, LANES * (n + 1))
        here = [own_ref[part, :, lanes] for part in range(3)]
        above = [
            jnp.concatenate([up_ref[part, :, lanes], here[part][:TILE]], 0) for part in range(3)
        ]
        below = [
            jnp.concatenate([here[part][TILE:], down_ref[part, :, lanes]], 0) for part in range(3)
        ]
        real, imag = meet_tiles(here[2] + lift_height, (above, below), table_ref)
        for part, near in enumerate((real, imag)):
            spectral = same_ref[0, part, :, lanes] + mate_ref[0, part, :, lanes]
            out_ref[part, :, lanes] = spectral + (side_ref[part, :, lanes] + area_weight * near)


def all_to_all_x(messages):
    shaped = messages.reshape(DEV_X, 1, 3 * LANES)
    moved = lax.all_to_all(shaped, "gx", split_axis=0, concat_axis=0, tiled=True)
    return moved.reshape(3 * DEV_X, LANES)


def local(unknown, height, spectrum_flat, spectrum_slope, spectrum_curve):
    mate_pairs = [(g, g ^ 1) for g in range(DEV_Y)]
    far_pairs = [(g, g ^ 2) for g in range(DEV_Y)]
    own, row_first, row_twist, outer = call(
        pack_kernel,
        (
            f32(3, ROWS, SPAN),
            held(2, LANES, LANES),
            held(2, HALF, LANES),
            held(2, LANES, 2 * LANES),
        ),
        unknown,
        height,
        TABLES["row_first"],
        TABLES["row_twist"],
        TABLES["outer"],
        loose=5,
        scratch=[pltpu.SemaphoreType.DMA((5,))],
    )
    far = lax.ppermute(own, "gy", far_pairs)
    mate = lax.ppermute(own, "gy", mate_pairs)
    diagonal = lax.ppermute(far, "gy", mate_pairs)
    groups = (own, far, mate, diagonal)
    sent, low = call(
        row_kernel,
        (f32(3 * DEV_X, LANES), f32(3, TILE, SPAN)),
        *groups,
        row_first,
        row_twist,
        outer,
    )
    arrived = all_to_all_x(sent)
    lined = [
        s.reshape(2, 64, LANES).transpose(1, 0, 2).reshape(2 * 64, LANES)
        for s in (spectrum_flat, spectrum_slope, spectrum_curve)
    ]
    spread, col_twist, col_small = call(
        spread_kernel,
        (
            held(6, LANES, LANES),
            held(2, LANES, LANES),
            held(2, 2, LANES, LANES),
        ),
        *lined,
        TABLES["col_twist"],
        TABLES["col_small"],
        sent,
        loose=5,
        waits=1,
        scratch=[
            pltpu.VMEM((3, LANES, LANES), jnp.float32),
            pltpu.SemaphoreType.DMA((5,)),
        ],
        flops=10_000_000,
    )
    up = lax.ppermute(low, "gx", [(i, (i + 1) % DEV_X) for i in range(DEV_X)])
    back, high = call(
        column_kernel,
        (f32(3 * DEV_X, LANES), f32(3, TILE, SPAN)),
        arrived,
        spread,
        outer,
        col_twist,
        col_small,
        own,
        up,
        waits=1,
    )
    down = lax.ppermute(high, "gx", [((i + 1) % DEV_X, i) for i in range(DEV_X)])
    returned = all_to_all_x(back)
    side, back_twist, back_last = call(
        side_kernel,
        (held(2, ROWS, SPAN), held(2, LANES, LANES), held(2, LANES, LANES)),
        *groups,
        SIDE_TABLE,
        TABLES["back_twist"],
        TABLES["back_last"],
        back,
        loose=2,
        waits=1,
        scratch=[
            pltpu.VMEM((SUBS + 2, 3, ROWS, LANES), jnp.float32),
            pltpu.SemaphoreType.DMA((2,)),
        ],
        flops=30_000_000,
    )
    same, crossed = call(
        inverse_kernel,
        (f32(2, 2, ROWS, SPAN), f32(2, 2, ROWS, SPAN)),
        returned,
        *groups,
        outer,
        back_twist,
        back_last,
        down,
        waits=1,
    )
    from_mate = lax.ppermute(crossed, "gy", mate_pairs)
    from_far = lax.ppermute(same[1] + from_mate[1], "gy", far_pairs)
    base = call(
        over_kernel,
        f32(2, ROWS, SPAN),
        own,
        up,
        down,
        OVER_TABLE,
        side,
        same,
        from_mate,
        flops=20_000_000,
    )
    return base + from_far


def solution(mesh):
    return jax.shard_map(
        local,
        mesh=mesh,
        in_specs=(
            P(None, "gx", "gy"),
            P("gx", "gy"),
            P(None, ("gx", "gy")),
            P(None, ("gx", "gy")),
            P(None, ("gx", "gy")),
        ),
        out_specs=P(None, "gx", "gy"),
        check_vma=False,
    )
```

```python
import functools
import math

import jax
import jax.numpy as jnp
import ml_dtypes
import numpy as np
from jax import lax
from jax.experimental import pallas as pl
from jax.experimental.pallas import tpu as pltpu
from jax.sharding import PartitionSpec as P

TILE = 4
wave_number = 2.0 * math.pi
spacing = 0.1
lift_height = 0.05
area_weight = spacing * spacing

ROWS = 8
SPAN = 1024
DEV_X = 128
DEV_Y = 4
LANES = 128
SUBS = SPAN // LANES
NARROW = 8
NX = ROWS * DEV_X
NY = SPAN * DEV_Y
HALF = ROWS * NARROW


def real_form(coeff):
    return np.block([[coeff.real, -coeff.imag], [coeff.imag, coeff.real]])


def halves(matrix):
    high = matrix.astype(ml_dtypes.bfloat16).astype(np.float64)
    low = (matrix - high).astype(ml_dtypes.bfloat16).astype(np.float64)
    return np.stack([high, low]).astype(np.float32)


def make_tables():
    r8 = np.arange(8)
    lane = np.arange(LANES)
    eye = np.eye(8)
    row_first, row_twist, back_twist, back_last = [], [], [], []
    for q in range(DEV_Y):
        small = np.exp(-2j * np.pi * (np.outer(r8, r8) / 8 + r8[None, :] * q / 32))
        grown = np.einsum("cn,rs->rcns", small, eye).reshape(HALF, HALF)
        row_first.append(real_form(grown))
        phase = np.exp(-2j * np.pi * lane[None, :] * (r8[:, None] / 1024 + q / 4096))
        phase = np.tile(phase, (8, 1))
        row_twist.append(np.stack([phase.real, phase.imag]))
        turn = phase.conj().T
        back_twist.append(
            np.stack(
                [
                    np.concatenate([turn.real, turn.real], 1),
                    np.concatenate([-turn.imag, turn.imag], 1),
                ]
            )
        )
        wide = np.einsum("cn,rs->nrsc", small.conj(), eye).reshape(HALF, HALF)
        back_last.append(real_form(wide))
    ring = 2 * np.pi * np.outer(lane, lane) / LANES
    outer = np.concatenate([np.cos(ring), np.sin(ring)], 1)
    turn = np.exp(-2j * np.pi * np.outer(lane, np.repeat(r8, NARROW)) / NX)
    col_twist = np.stack(
        [
            np.concatenate([turn.real, turn.real], 1),
            np.concatenate([-turn.imag, turn.imag], 1),
        ]
    )
    ring8 = np.exp(-2j * np.pi * np.outer(r8, r8) / 8)
    grown = np.kron(ring8, np.eye(NARROW))
    col_small = real_form(grown).T
    col_back = real_form(grown.conj().T).T / (NX * NY)
    as32 = lambda x: np.asarray(x, np.float32)
    return {
        "row_first": np.stack([halves(x) for x in row_first]),
        "row_twist": as32(np.stack(row_twist)),
        "outer": halves(outer),
        "col_twist": as32(col_twist),
        "col_small": np.stack([halves(col_small), halves(col_back)]),
        "back_twist": as32(np.stack(back_twist)),
        "back_last": np.stack([halves(x) for x in back_last]),
    }


TABLES = make_tables()


def parts_of(x):
    high = x.astype(jnp.bfloat16)
    return high, (x - high.astype(jnp.float32)).astype(jnp.bfloat16)


def product(left, right, dims):
    def one(x, y):
        return lax.dot_general(x, y, (dims, ((), ())), preferred_element_type=jnp.float32)

    return one(left[0], right[0]) + (one(left[0], right[1]) + one(left[1], right[0]))


def dot(left, right):
    return product(left, right, ((1,), (0,)))


def dot_t(left, right):
    return product(left, right, ((1,), (1,)))


def table_parts(ref):
    return ref[0].astype(jnp.bfloat16), ref[1].astype(jnp.bfloat16)


def tiles_of(cells):
    return jnp.concatenate([cells[:, LANES * n : LANES * (n + 1)] for n in range(SUBS)], 0)


def swap_halves(x, sign):
    return pltpu.roll(x, 64, 1) * sign


def half_sign(first, second):
    lane = lax.broadcasted_iota(jnp.int32, (LANES, LANES), 1)
    return jnp.where(lane < 64, jnp.float32(first), jnp.float32(second))


def quarter_turn(k, direction):
    k = k % 4
    real = jnp.where(k == 0, 1.0, jnp.where(k == 2, -1.0, 0.0)).astype(jnp.float32)
    imag = jnp.where(k == 1, direction, jnp.where(k == 3, -direction, 0.0)).astype(jnp.float32)
    return real, imag


def parity_sign(q):
    return jnp.where(q % 2 == 0, 1.0, -1.0).astype(jnp.float32)


def row_spectra(q, blocks, first, twist, outer):
    sign = parity_sign(q)
    own_real, own_imag = quarter_turn(q * q, -1.0)
    mate_real, mate_imag = quarter_turn((q ^ 1) * q, -1.0)
    powers = []
    for real, imag, height in blocks:
        levels = [(real, imag)]
        for _ in range(2):
            levels.append((levels[-1][0] * height, levels[-1][1] * height))
        powers.append(levels)
    stacked = []
    for b in range(3):
        same = [powers[0][b][k] + sign * powers[1][b][k] for k in range(2)]
        mate = [powers[2][b][k] + sign * powers[3][b][k] for k in range(2)]
        merged_real = (own_real * same[0] - own_imag * same[1]) + (
            mate_real * mate[0] - mate_imag * mate[1]
        )
        merged_imag = (own_real * same[1] + own_imag * same[0]) + (
            mate_real * mate[1] + mate_imag * mate[0]
        )
        stacked.append(jnp.concatenate([merged_real, merged_imag], 0))
    stepped = dot(first, parts_of(jnp.concatenate(stacked, 1)))
    turned = []
    for b in range(3):
        part = stepped[:, LANES * b : LANES * (b + 1)]
        real, imag = part[:HALF], part[HALF:]
        z_real = real * twist[0] - imag * twist[1]
        z_imag = real * twist[1] + imag * twist[0]
        turned.append(
            jnp.concatenate(
                [
                    jnp.concatenate([z_real, z_imag], 1),
                    jnp.concatenate([z_imag, -z_real], 1),
                ],
                0,
            )
        )
    return dot_t(outer, parts_of(jnp.concatenate(turned, 0)))


def column_stage(blocks, kernels, outer, twist, small, small_back):
    plus_minus = half_sign(1.0, -1.0)
    minus_plus = half_sign(-1.0, 1.0)
    lower = [swap_halves(x, plus_minus) for x in blocks]
    stepped = dot(
        outer,
        parts_of(jnp.concatenate([jnp.concatenate(blocks, 1), jnp.concatenate(lower, 1)], 0)),
    )
    turned = []
    for b in range(3):
        part = stepped[:, LANES * b : LANES * (b + 1)]
        turned.append(part * twist[0] + pltpu.roll(part, 64, 1) * twist[1])
    spectra = dot(parts_of(jnp.concatenate(turned, 0)), small)
    plain = [spectra[LANES * b : LANES * (b + 1)] for b in range(3)]
    rolled = [pltpu.roll(x, 64, 1) for x in plain]

    def times(m, b):
        return kernels[m][0] * plain[b] + kernels[m][1] * rolled[b]

    mixed = [
        times(0, 0) - times(1, 1) + times(2, 2),
        times(1, 0) - 2.0 * times(2, 1),
        times(2, 0),
    ]
    back = dot(parts_of(jnp.concatenate(mixed, 0)), small_back)
    upper, under = [], []
    for a in range(3):
        part = back[LANES * a : LANES * (a + 1)]
        turned = part * twist[0] - pltpu.roll(part, 64, 1) * twist[1]
        upper.append(turned)
        under.append(swap_halves(turned, minus_plus))
    return dot(
        outer, parts_of(jnp.concatenate([jnp.concatenate(upper, 1), jnp.concatenate(under, 1)], 0))
    )


def row_inverse(q, blocks, heights, outer, twist, last):
    minus_plus = half_sign(-1.0, 1.0)
    under = [swap_halves(x, minus_plus) for x in blocks]
    stepped = dot(
        outer,
        parts_of(jnp.concatenate([jnp.concatenate(blocks, 1), jnp.concatenate(under, 1)], 0)),
    )
    turned = []
    for a in range(3):
        part = stepped[:, LANES * a : LANES * (a + 1)]
        turned.append(part * twist[0] + pltpu.roll(part, 64, 1) * twist[1])
    fields = dot_t(last, parts_of(jnp.concatenate(turned, 0)))
    level = [fields[:, LANES * a : LANES * (a + 1)] for a in range(3)]
    sums = []
    for m, height in zip((0, 2, 1, 3), heights):
        scale_real, scale_imag = quarter_turn((q ^ m) * q, 1.0)
        real = (level[2][:HALF] * height + level[1][:HALF]) * height + level[0][:HALF]
        imag = (level[2][HALF:] * height + level[1][HALF:]) * height + level[0][HALF:]
        sums.append((scale_real * real - scale_imag * imag, scale_real * imag + scale_imag * real))
    return sums


vmem = pl.BlockSpec(memory_space=pltpu.VMEM)


def call(body, shapes, *args, loose=0, waits=0, scratch=(), flops=1_000_000, moved=1_000_000):
    blocks = len(args) - loose - waits
    specs = [vmem] * blocks + [pl.BlockSpec(memory_space=pl.ANY)] * (loose + waits)
    kept = list(args)
    for n in range(blocks, blocks + loose):
        kept[n] = pltpu.with_memory_space_constraint(jnp.asarray(args[n]), pltpu.HBM)
    return pl.pallas_call(
        body,
        out_shape=shapes,
        in_specs=specs,
        out_specs=jax.tree.map(lambda _: vmem, shapes),
        scratch_shapes=scratch,
        compiler_params=pltpu.CompilerParams(vmem_limit_bytes=40 * 1024 * 1024),
        cost_estimate=pl.CostEstimate(flops=flops, bytes_accessed=moved, transcendentals=0),
    )(*kept)


def held(*shape):
    return pltpu.VMEM(shape, jnp.float32)


def f32(*shape):
    return jax.ShapeDtypeStruct(shape, jnp.float32)


def fetch(pairs, sems):
    copies = [pltpu.make_async_copy(src, dst, sems.at[n]) for n, (src, dst) in enumerate(pairs)]
    for copy in copies:
        copy.start()
    return copies


def pack_kernel(
    unknown_ref, height_ref, first_ref, twist_ref, outer_ref, own_ref, first_out, twist_out, outer_out, sems
):
    q = lax.axis_index("gy")
    copies = fetch(
        [
            (unknown_ref, own_ref.at[pl.ds(0, 2)]),
            (height_ref, own_ref.at[2]),
            (first_ref.at[q], first_out),
            (twist_ref.at[q], twist_out),
            (outer_ref, outer_out),
        ],
        sems,
    )
    for copy in copies:
        copy.wait()


def row_kernel(
    own_ref, far_ref, mate_ref, diag_ref, first_ref, twist_ref, outer_ref, out_ref, low_ref
):
    q = lax.axis_index("gy")
    blocks = [
        [tiles_of(ref[part]) for part in range(3)] for ref in (own_ref, far_ref, mate_ref, diag_ref)
    ]
    out = row_spectra(q, blocks, table_parts(first_ref), twist_ref, table_parts(outer_ref))
    for b in range(3):
        out_ref[pl.ds(b, DEV_X, stride=3), :] = out[:, LANES * b : LANES * (b + 1)]
    low_ref[...] = own_ref[:, TILE:]


def spread_spectra(refs, out_ref):
    lane = lax.broadcasted_iota(jnp.int32, (64, LANES), 1)
    for m, ref in enumerate(refs):
        real = ref[pl.ds(0, 64, stride=2), :]
        imag = ref[pl.ds(1, 64, stride=2), :]
        for parity in range(2):
            low = lane < 64 if parity == 0 else lane >= 64
            both_real = jnp.where(low, real, pltpu.roll(real, 64, 1))
            both_imag = jnp.where(low, imag, pltpu.roll(imag, 64, 1))
            out_ref[2 * m, pl.ds(parity, 64, stride=2), :] = both_real
            out_ref[2 * m + 1, pl.ds(parity, 64, stride=2), :] = jnp.where(
                lane < 64, -both_imag, both_imag
            )


def column_kernel(
    in_ref, spread_ref, outer_ref, twist_ref, small_ref, own_ref, side_ref, out_ref, high_ref
):
    blocks = [in_ref[pl.ds(b, DEV_X, stride=3), :] for b in range(3)]
    kernels = [(spread_ref[2 * m], spread_ref[2 * m + 1]) for m in range(3)]
    out = column_stage(
        blocks,
        kernels,
        table_parts(outer_ref),
        twist_ref,
        table_parts(small_ref.at[0]),
        table_parts(small_ref.at[1]),
    )
    for a in range(3):
        out_ref[pl.ds(a, DEV_X, stride=3), :] = out[:, LANES * a : LANES * (a + 1)]
    high_ref[...] = own_ref[:, :TILE]


def inverse_kernel(
    in_ref,
    own_ref,
    far_ref,
    mate_ref,
    diag_ref,
    outer_ref,
    twist_ref,
    last_ref,
    up_ref,
    down_ref,
    same_ref,
    crossed_ref,
):
    q = lax.axis_index("gy")
    blocks = [in_ref[pl.ds(a, DEV_X, stride=3), :] for a in range(3)]
    heights = [tiles_of(ref[2]) for ref in (own_ref, far_ref, mate_ref, diag_ref)]
    sums = row_inverse(
        q, blocks, heights, table_parts(outer_ref), twist_ref, table_parts(last_ref)
    )
    places = ((same_ref, 0), (same_ref, 1), (crossed_ref, 0), (crossed_ref, 1))
    for (ref, slot), pair in zip(places, sums):
        for part in range(2):
            for n in range(SUBS):
                ref[slot, part, :, LANES * n : LANES * (n + 1)] = pair[part][
                    ROWS * n : ROWS * (n + 1)
                ]


X_TOP = 1.31


def fit(function, degree):
    cheb = np.polynomial.chebyshev.Chebyshev.interpolate(function, degree, [0.0, X_TOP])
    power = cheb.convert(kind=np.polynomial.Polynomial, domain=[-1, 1], window=[-1, 1])
    moved = power(np.polynomial.Polynomial([X_TOP / 2, 1.0]))
    return [float(c) for c in moved.coef[::-1]]


COS_FIT = fit(lambda x: np.cos(wave_number * np.sqrt(x)), 9)
SIN_FIT = fit(lambda x: wave_number * np.sinc(2.0 * np.sqrt(x)), 8)


def near_table(kinds):
    cell = np.arange(TILE)
    entries = []
    for shift_row, shift_col in kinds:
        for sr in range(TILE):
            for sc in range(TILE):
                dr = (cell + sr) % TILE - cell + TILE * shift_row
                dc = (cell + sc) % TILE - cell + TILE * shift_col
                rho2 = spacing * spacing * (dr[:, None] ** 2 + dc[None, :] ** 2)
                radius = np.sqrt(rho2 + lift_height**2)
                green = np.exp(1j * wave_number * radius) / radius
                log_slope = 1j * wave_number - 1 / radius
                first_r = green * log_slope
                second_r = green * (log_slope**2 + 1 / radius**2)
                rise = lift_height / radius
                k1 = first_r * rise
                k2 = 0.5 * (second_r * rise**2 + first_r * (1 - rise**2) / radius)
                a0 = green - lift_height * k1 + lift_height**2 * k2
                a1 = k1 - 2 * lift_height * k2
                offset = rho2 - X_TOP / 2
                line = SIN_FIT[-2] - k2.imag
                level = SIN_FIT[-1] - a0.imag + k2.imag * offset
                entry = [offset, a0.real, a1.real, k2.real, level, line, a1.imag]
                entries.append([np.tile(e, (ROWS // TILE, LANES // TILE)) for e in entry])
    return np.asarray(entries, np.float32)


SIDE_KINDS = ((0, 0), (0, -1), (0, 1))
OVER_KINDS = ((-1, 0), (1, 0))
SIDE_TABLE = near_table(SIDE_KINDS)
OVER_TABLE = near_table(OVER_KINDS)


def horner(coefficients, x):
    total = coefficients[0] * x + coefficients[1]
    for c in coefficients[2:]:
        total = total * x + c
    return total


def turned_index(axis, turn):
    place = lax.broadcasted_iota(jnp.int32, (ROWS, LANES), axis)
    within = place % TILE
    return place - within + (within + turn) % TILE


def turn_cells(x, axis, turn):
    if turn == 0:
        return x
    return jnp.take_along_axis(x, turned_index(axis, turn), axis=axis)


def meet(raised, source, table_ref, entry):
    real, imag, height = source
    w = raised - height
    v = w * w
    u = v + table_ref[entry, 0]
    root = lax.rsqrt(u + X_TOP / 2)
    gap_real = horner(COS_FIT, u) * root - (
        table_ref[entry, 2] * w + (table_ref[entry, 3] * v + table_ref[entry, 1])
    )
    fitted = (horner(SIN_FIT[:-2], u) * u + table_ref[entry, 5]) * u + table_ref[entry, 4]
    gap_imag = fitted - table_ref[entry, 6] * w
    return gap_real * real - gap_imag * imag, gap_real * imag + gap_imag * real


def meet_tiles(raised, sources, table_ref):
    total_real = jnp.zeros((ROWS, LANES), jnp.float32)
    total_imag = jnp.zeros((ROWS, LANES), jnp.float32)
    for kind, source in enumerate(sources):
        for sc in range(TILE):
            column = [turn_cells(x, 1, sc) for x in source]
            for sr in range(TILE):
                cells = [turn_cells(x, 0, sr) for x in column]
                entry = (kind * TILE + sr) * TILE + sc
                real, imag = meet(raised, cells, table_ref, entry)
                total_real = total_real + real
                total_imag = total_imag + imag
    return total_real, total_imag


def spread_kernel(
    flat_ref,
    slope_ref,
    curve_ref,
    twist_ref,
    small_ref,
    after_ref,
    spread_ref,
    twist_out,
    small_out,
    lined,
    sems,
):
    copies = fetch(
        [
            (flat_ref, lined.at[0]),
            (slope_ref, lined.at[1]),
            (curve_ref, lined.at[2]),
            (twist_ref, twist_out),
            (small_ref, small_out),
        ],
        sems,
    )
    for copy in copies:
        copy.wait()
    spread_spectra([lined.at[m] for m in range(3)], spread_ref)


def side_kernel(
    own_ref,
    far_ref,
    mate_ref,
    diag_ref,
    table_ref,
    back_twist_ref,
    back_last_ref,
    after_ref,
    out_ref,
    back_twist_out,
    back_last_out,
    edge,
    sems,
):
    q = lax.axis_index("gy")
    copies = fetch(
        [(back_twist_ref.at[q], back_twist_out), (back_last_ref.at[q], back_last_out)], sems
    )
    odd = q % 2 == 1
    for part in range(3):
        last = slice(SPAN - LANES, SPAN)
        first = slice(0, LANES)
        edge[0, part] = jnp.where(odd, mate_ref[part, :, last], diag_ref[part, :, last])
        edge[SUBS + 1, part] = jnp.where(odd, diag_ref[part, :, first], mate_ref[part, :, first])
        for n in range(SUBS):
            edge[n + 1, part] = own_ref[part, :, LANES * n : LANES * (n + 1)]
    lane = lax.broadcasted_iota(jnp.int32, (ROWS, LANES), 1)

    for n in range(SUBS):
        before = [edge[n, part] for part in range(3)]
        here = [edge[n + 1, part] for part in range(3)]
        after = [edge[n + 2, part] for part in range(3)]
        left = [
            jnp.where(lane < TILE, pltpu.roll(x, TILE, 1), pltpu.roll(y, TILE, 1))
            for x, y in zip(before, here)
        ]
        right = [
            jnp.where(
                lane < LANES - TILE,
                pltpu.roll(y, LANES - TILE, 1),
                pltpu.roll(z, LANES - TILE, 1),
            )
            for y, z in zip(here, after)
        ]
        real, imag = meet_tiles(here[2] + lift_height, (here, left, right), table_ref)
        out_ref[0, :, LANES * n : LANES * (n + 1)] = area_weight * real
        out_ref[1, :, LANES * n : LANES * (n + 1)] = area_weight * imag
    for copy in copies:
        copy.wait()


def over_kernel(own_ref, up_ref, down_ref, table_ref, side_ref, same_ref, mate_ref, out_ref):
    for n in range(SUBS):
        lanes = slice(LANES * n, LANES * (n + 1))
        here = [own_ref[part, :, lanes] for part in range(3)]
        above = [
            jnp.concatenate([up_ref[part, :, lanes], here[part][:TILE]], 0) for part in range(3)
        ]
        below = [
            jnp.concatenate([here[part][TILE:], down_ref[part, :, lanes]], 0) for part in range(3)
        ]
        real, imag = meet_tiles(here[2] + lift_height, (above, below), table_ref)
        for part, near in enumerate((real, imag)):
            spectral = same_ref[0, part, :, lanes] + mate_ref[0, part, :, lanes]
            out_ref[part, :, lanes] = spectral + (side_ref[part, :, lanes] + area_weight * near)


def all_to_all_x(messages):
    shaped = messages.reshape(DEV_X, 1, 3 * LANES)
    moved = lax.all_to_all(shaped, "gx", split_axis=0, concat_axis=0, tiled=True)
    return moved.reshape(3 * DEV_X, LANES)


def local(unknown, height, spectrum_flat, spectrum_slope, spectrum_curve):
    mate_pairs = [(g, g ^ 1) for g in range(DEV_Y)]
    far_pairs = [(g, g ^ 2) for g in range(DEV_Y)]
    own, row_first, row_twist, outer = call(
        pack_kernel,
        (
            f32(3, ROWS, SPAN),
            held(2, LANES, LANES),
            held(2, HALF, LANES),
            held(2, LANES, 2 * LANES),
        ),
        unknown,
        height,
        TABLES["row_first"],
        TABLES["row_twist"],
        TABLES["outer"],
        loose=5,
        scratch=[pltpu.SemaphoreType.DMA((5,))],
    )
    far = lax.ppermute(own, "gy", far_pairs)
    mate = lax.ppermute(own, "gy", mate_pairs)
    diagonal = lax.ppermute(far, "gy", mate_pairs)
    groups = (own, far, mate, diagonal)
    sent, low = call(
        row_kernel,
        (f32(3 * DEV_X, LANES), f32(3, TILE, SPAN)),
        *groups,
        row_first,
        row_twist,
        outer,
    )
    arrived = all_to_all_x(sent)
    lined = [
        s.reshape(2, 64, LANES).transpose(1, 0, 2).reshape(2 * 64, LANES)
        for s in (spectrum_flat, spectrum_slope, spectrum_curve)
    ]
    spread, col_twist, col_small = call(
        spread_kernel,
        (
            held(6, LANES, LANES),
            held(2, LANES, LANES),
            held(2, 2, LANES, LANES),
        ),
        *lined,
        TABLES["col_twist"],
        TABLES["col_small"],
        sent,
        loose=5,
        waits=1,
        scratch=[
            pltpu.VMEM((3, LANES, LANES), jnp.float32),
            pltpu.SemaphoreType.DMA((5,)),
        ],
        flops=10_000_000,
    )
    up = lax.ppermute(low, "gx", [(i, (i + 1) % DEV_X) for i in range(DEV_X)])
    side, back_twist, back_last = call(
        side_kernel,
        (held(2, ROWS, SPAN), held(2, LANES, LANES), held(2, LANES, LANES)),
        *groups,
        SIDE_TABLE,
        TABLES["back_twist"],
        TABLES["back_last"],
        spread,
        loose=2,
        waits=1,
        scratch=[
            pltpu.VMEM((SUBS + 2, 3, ROWS, LANES), jnp.float32),
            pltpu.SemaphoreType.DMA((2,)),
        ],
        flops=30_000_000,
    )
    back, high = call(
        column_kernel,
        (f32(3 * DEV_X, LANES), f32(3, TILE, SPAN)),
        arrived,
        spread,
        outer,
        col_twist,
        col_small,
        own,
        side,
        waits=1,
    )
    down = lax.ppermute(high, "gx", [((i + 1) % DEV_X, i) for i in range(DEV_X)])
    returned = all_to_all_x(back)
    same, crossed = call(
        inverse_kernel,
        (f32(2, 2, ROWS, SPAN), f32(2, 2, ROWS, SPAN)),
        returned,
        *groups,
        outer,
        back_twist,
        back_last,
        up,
        down,
        waits=2,
    )
    from_mate = lax.ppermute(crossed, "gy", mate_pairs)
    from_far = lax.ppermute(same[1] + from_mate[1], "gy", far_pairs)
    base = call(
        over_kernel,
        f32(2, ROWS, SPAN),
        own,
        up,
        down,
        OVER_TABLE,
        side,
        same,
        from_mate,
        flops=20_000_000,
    )
    return base + from_far


def solution(mesh):
    return jax.shard_map(
        local,
        mesh=mesh,
        in_specs=(
            P(None, "gx", "gy"),
            P("gx", "gy"),
            P(None, ("gx", "gy")),
            P(None, ("gx", "gy")),
            P(None, ("gx", "gy")),
        ),
        out_specs=P(None, "gx", "gy"),
        check_vma=False,
    )
```

```python
import functools
import math

import jax
import jax.numpy as jnp
import ml_dtypes
import numpy as np
from jax import lax
from jax.experimental import pallas as pl
from jax.experimental.pallas import tpu as pltpu
from jax.sharding import PartitionSpec as P

TILE = 4
wave_number = 2.0 * math.pi
spacing = 0.1
lift_height = 0.05
area_weight = spacing * spacing

ROWS = 8
SPAN = 1024
DEV_X = 128
DEV_Y = 4
LANES = 128
SUBS = SPAN // LANES
NARROW = 8
NX = ROWS * DEV_X
NY = SPAN * DEV_Y
HALF = ROWS * NARROW


def real_form(coeff):
    return np.block([[coeff.real, -coeff.imag], [coeff.imag, coeff.real]])


def halves(matrix):
    high = matrix.astype(ml_dtypes.bfloat16).astype(np.float64)
    low = (matrix - high).astype(ml_dtypes.bfloat16).astype(np.float64)
    return np.stack([high, low]).astype(np.float32)


def make_tables():
    r8 = np.arange(8)
    lane = np.arange(LANES)
    eye = np.eye(8)
    row_first, row_twist, back_twist, back_last = [], [], [], []
    for q in range(DEV_Y):
        small = np.exp(-2j * np.pi * (np.outer(r8, r8) / 8 + r8[None, :] * q / 32))
        grown = np.einsum("cn,rs->rcns", small, eye).reshape(HALF, HALF)
        row_first.append(real_form(grown))
        phase = np.exp(-2j * np.pi * lane[None, :] * (r8[:, None] / 1024 + q / 4096))
        phase = np.tile(phase, (8, 1))
        row_twist.append(np.stack([phase.real, phase.imag]))
        turn = phase.conj().T
        back_twist.append(
            np.stack(
                [
                    np.concatenate([turn.real, turn.real], 1),
                    np.concatenate([-turn.imag, turn.imag], 1),
                ]
            )
        )
        wide = np.einsum("cn,rs->nrsc", small.conj(), eye).reshape(HALF, HALF)
        back_last.append(real_form(wide))
    ring = 2 * np.pi * np.outer(lane, lane) / LANES
    outer = np.concatenate([np.cos(ring), np.sin(ring)], 1)
    turn = np.exp(-2j * np.pi * np.outer(lane, np.repeat(r8, NARROW)) / NX)
    col_twist = np.stack(
        [
            np.concatenate([turn.real, turn.real], 1),
            np.concatenate([-turn.imag, turn.imag], 1),
        ]
    )
    ring8 = np.exp(-2j * np.pi * np.outer(r8, r8) / 8)
    grown = np.kron(ring8, np.eye(NARROW))
    col_small = real_form(grown).T
    col_back = real_form(grown.conj().T).T / (NX * NY)
    as32 = lambda x: np.asarray(x, np.float32)
    return {
        "row_first": np.stack([halves(x) for x in row_first]),
        "row_twist": as32(np.stack(row_twist)),
        "outer": halves(outer),
        "col_twist": as32(col_twist),
        "col_small": np.stack([halves(col_small), halves(col_back)]),
        "back_twist": as32(np.stack(back_twist)),
        "back_last": np.stack([halves(x) for x in back_last]),
    }


TABLES = make_tables()


def parts_of(x):
    high = x.astype(jnp.bfloat16)
    return high, (x - high.astype(jnp.float32)).astype(jnp.bfloat16)


def product(left, right, dims):
    def one(x, y):
        return lax.dot_general(x, y, (dims, ((), ())), preferred_element_type=jnp.float32)

    rows = left[0].shape[0]
    both = one(jnp.concatenate(left, 0), right[0])
    return both[:rows] + (one(left[0], right[1]) + both[rows:])


def dot(left, right):
    return product(left, right, ((1,), (0,)))


def dot_t(left, right):
    return product(left, right, ((1,), (1,)))


def table_parts(ref):
    return ref[0].astype(jnp.bfloat16), ref[1].astype(jnp.bfloat16)


def tiles_of(cells):
    return jnp.concatenate([cells[:, LANES * n : LANES * (n + 1)] for n in range(SUBS)], 0)


def swap_halves(x, sign):
    return pltpu.roll(x, 64, 1) * sign


def half_sign(first, second):
    lane = lax.broadcasted_iota(jnp.int32, (LANES, LANES), 1)
    return jnp.where(lane < 64, jnp.float32(first), jnp.float32(second))


def quarter_turn(k, direction):
    k = k % 4
    real = jnp.where(k == 0, 1.0, jnp.where(k == 2, -1.0, 0.0)).astype(jnp.float32)
    imag = jnp.where(k == 1, direction, jnp.where(k == 3, -direction, 0.0)).astype(jnp.float32)
    return real, imag


def parity_sign(q):
    return jnp.where(q % 2 == 0, 1.0, -1.0).astype(jnp.float32)


def row_spectra(q, blocks, first, twist, outer):
    sign = parity_sign(q)
    own_real, own_imag = quarter_turn(q * q, -1.0)
    mate_real, mate_imag = quarter_turn((q ^ 1) * q, -1.0)
    powers = []
    for real, imag, height in blocks:
        levels = [(real, imag)]
        for _ in range(2):
            levels.append((levels[-1][0] * height, levels[-1][1] * height))
        powers.append(levels)
    stacked = []
    for b in range(3):
        same = [powers[0][b][k] + sign * powers[1][b][k] for k in range(2)]
        mate = [powers[2][b][k] + sign * powers[3][b][k] for k in range(2)]
        merged_real = (own_real * same[0] - own_imag * same[1]) + (
            mate_real * mate[0] - mate_imag * mate[1]
        )
        merged_imag = (own_real * same[1] + own_imag * same[0]) + (
            mate_real * mate[1] + mate_imag * mate[0]
        )
        stacked.append(jnp.concatenate([merged_real, merged_imag], 0))
    stepped = dot(first, parts_of(jnp.concatenate(stacked, 1)))
    turned = []
    for b in range(3):
        part = stepped[:, LANES * b : LANES * (b + 1)]
        real, imag = part[:HALF], part[HALF:]
        z_real = real * twist[0] - imag * twist[1]
        z_imag = real * twist[1] + imag * twist[0]
        turned.append(
            jnp.concatenate(
                [
                    jnp.concatenate([z_real, z_imag], 1),
                    jnp.concatenate([z_imag, -z_real], 1),
                ],
                0,
            )
        )
    return dot_t(outer, parts_of(jnp.concatenate(turned, 0)))


def column_stage(blocks, kernels, outer, twist, small, small_back):
    plus_minus = half_sign(1.0, -1.0)
    minus_plus = half_sign(-1.0, 1.0)
    lower = [swap_halves(x, plus_minus) for x in blocks]
    stepped = dot(
        outer,
        parts_of(jnp.concatenate([jnp.concatenate(blocks, 1), jnp.concatenate(lower, 1)], 0)),
    )
    turned = []
    for b in range(3):
        part = stepped[:, LANES * b : LANES * (b + 1)]
        turned.append(part * twist[0] + pltpu.roll(part, 64, 1) * twist[1])
    spectra = dot(parts_of(jnp.concatenate(turned, 0)), small)
    plain = [spectra[LANES * b : LANES * (b + 1)] for b in range(3)]
    rolled = [pltpu.roll(x, 64, 1) for x in plain]

    def times(m, b):
        return kernels[m][0] * plain[b] + kernels[m][1] * rolled[b]

    mixed = [
        times(0, 0) - times(1, 1) + times(2, 2),
        times(1, 0) - 2.0 * times(2, 1),
        times(2, 0),
    ]
    back = dot(parts_of(jnp.concatenate(mixed, 0)), small_back)
    upper, under = [], []
    for a in range(3):
        part = back[LANES * a : LANES * (a + 1)]
        turned = part * twist[0] - pltpu.roll(part, 64, 1) * twist[1]
        upper.append(turned)
        under.append(swap_halves(turned, minus_plus))
    return dot(
        outer, parts_of(jnp.concatenate([jnp.concatenate(upper, 1), jnp.concatenate(under, 1)], 0))
    )


def row_inverse(q, blocks, heights, outer, twist, last):
    minus_plus = half_sign(-1.0, 1.0)
    under = [swap_halves(x, minus_plus) for x in blocks]
    stepped = dot(
        outer,
        parts_of(jnp.concatenate([jnp.concatenate(blocks, 1), jnp.concatenate(under, 1)], 0)),
    )
    turned = []
    for a in range(3):
        part = stepped[:, LANES * a : LANES * (a + 1)]
        turned.append(part * twist[0] + pltpu.roll(part, 64, 1) * twist[1])
    fields = dot_t(last, parts_of(jnp.concatenate(turned, 0)))
    level = [fields[:, LANES * a : LANES * (a + 1)] for a in range(3)]
    sums = []
    for m, height in zip((0, 2, 1, 3), heights):
        scale_real, scale_imag = quarter_turn((q ^ m) * q, 1.0)
        real = (level[2][:HALF] * height + level[1][:HALF]) * height + level[0][:HALF]
        imag = (level[2][HALF:] * height + level[1][HALF:]) * height + level[0][HALF:]
        sums.append((scale_real * real - scale_imag * imag, scale_real * imag + scale_imag * real))
    return sums


vmem = pl.BlockSpec(memory_space=pltpu.VMEM)


def call(body, shapes, *args, loose=0, waits=0, scratch=(), flops=1_000_000, moved=1_000_000):
    blocks = len(args) - loose - waits
    specs = [vmem] * blocks + [pl.BlockSpec(memory_space=pl.ANY)] * (loose + waits)
    kept = list(args)
    for n in range(blocks, blocks + loose):
        kept[n] = pltpu.with_memory_space_constraint(jnp.asarray(args[n]), pltpu.HBM)
    return pl.pallas_call(
        body,
        out_shape=shapes,
        in_specs=specs,
        out_specs=jax.tree.map(lambda _: vmem, shapes),
        scratch_shapes=scratch,
        compiler_params=pltpu.CompilerParams(vmem_limit_bytes=40 * 1024 * 1024),
        cost_estimate=pl.CostEstimate(flops=flops, bytes_accessed=moved, transcendentals=0),
    )(*kept)


def held(*shape):
    return pltpu.VMEM(shape, jnp.float32)


def f32(*shape):
    return jax.ShapeDtypeStruct(shape, jnp.float32)


def fetch(pairs, sems):
    copies = [pltpu.make_async_copy(src, dst, sems.at[n]) for n, (src, dst) in enumerate(pairs)]
    for copy in copies:
        copy.start()
    return copies


def pack_kernel(
    unknown_ref, height_ref, first_ref, twist_ref, outer_ref, own_ref, first_out, twist_out, outer_out, sems
):
    q = lax.axis_index("gy")
    copies = fetch(
        [
            (unknown_ref, own_ref.at[pl.ds(0, 2)]),
            (height_ref, own_ref.at[2]),
            (first_ref.at[q], first_out),
            (twist_ref.at[q], twist_out),
            (outer_ref, outer_out),
        ],
        sems,
    )
    for copy in copies:
        copy.wait()


def row_kernel(
    own_ref, far_ref, mate_ref, diag_ref, first_ref, twist_ref, outer_ref, out_ref, low_ref
):
    q = lax.axis_index("gy")
    blocks = [
        [tiles_of(ref[part]) for part in range(3)] for ref in (own_ref, far_ref, mate_ref, diag_ref)
    ]
    out = row_spectra(q, blocks, table_parts(first_ref), twist_ref, table_parts(outer_ref))
    for b in range(3):
        out_ref[pl.ds(b, DEV_X, stride=3), :] = out[:, LANES * b : LANES * (b + 1)]
    low_ref[...] = own_ref[:, TILE:]


def spread_spectra(refs, out_ref):
    lane = lax.broadcasted_iota(jnp.int32, (64, LANES), 1)
    for m, ref in enumerate(refs):
        real = ref[pl.ds(0, 64, stride=2), :]
        imag = ref[pl.ds(1, 64, stride=2), :]
        for parity in range(2):
            low = lane < 64 if parity == 0 else lane >= 64
            both_real = jnp.where(low, real, pltpu.roll(real, 64, 1))
            both_imag = jnp.where(low, imag, pltpu.roll(imag, 64, 1))
            out_ref[2 * m, pl.ds(parity, 64, stride=2), :] = both_real
            out_ref[2 * m + 1, pl.ds(parity, 64, stride=2), :] = jnp.where(
                lane < 64, -both_imag, both_imag
            )


def column_kernel(
    in_ref, spread_ref, outer_ref, twist_ref, small_ref, own_ref, side_ref, out_ref, high_ref
):
    blocks = [in_ref[pl.ds(b, DEV_X, stride=3), :] for b in range(3)]
    kernels = [(spread_ref[2 * m], spread_ref[2 * m + 1]) for m in range(3)]
    out = column_stage(
        blocks,
        kernels,
        table_parts(outer_ref),
        twist_ref,
        table_parts(small_ref.at[0]),
        table_parts(small_ref.at[1]),
    )
    for a in range(3):
        out_ref[pl.ds(a, DEV_X, stride=3), :] = out[:, LANES * a : LANES * (a + 1)]
    high_ref[...] = own_ref[:, :TILE]


def inverse_kernel(
    in_ref,
    own_ref,
    far_ref,
    mate_ref,
    diag_ref,
    outer_ref,
    twist_ref,
    last_ref,
    up_ref,
    down_ref,
    same_ref,
    crossed_ref,
):
    q = lax.axis_index("gy")
    blocks = [in_ref[pl.ds(a, DEV_X, stride=3), :] for a in range(3)]
    heights = [tiles_of(ref[2]) for ref in (own_ref, far_ref, mate_ref, diag_ref)]
    sums = row_inverse(
        q, blocks, heights, table_parts(outer_ref), twist_ref, table_parts(last_ref)
    )
    places = ((same_ref, 0), (same_ref, 1), (crossed_ref, 0), (crossed_ref, 1))
    for (ref, slot), pair in zip(places, sums):
        for part in range(2):
            for n in range(SUBS):
                ref[slot, part, :, LANES * n : LANES * (n + 1)] = pair[part][
                    ROWS * n : ROWS * (n + 1)
                ]


X_TOP = 1.31


def fit(function, degree):
    cheb = np.polynomial.chebyshev.Chebyshev.interpolate(function, degree, [0.0, X_TOP])
    power = cheb.convert(kind=np.polynomial.Polynomial, domain=[-1, 1], window=[-1, 1])
    moved = power(np.polynomial.Polynomial([X_TOP / 2, 1.0]))
    return [float(c) for c in moved.coef[::-1]]


COS_FIT = fit(lambda x: np.cos(wave_number * np.sqrt(x)), 9)
SIN_FIT = fit(lambda x: wave_number * np.sinc(2.0 * np.sqrt(x)), 8)


def near_table(kinds):
    cell = np.arange(TILE)
    entries = []
    for shift_row, shift_col in kinds:
        for sr in range(TILE):
            for sc in range(TILE):
                dr = (cell + sr) % TILE - cell + TILE * shift_row
                dc = (cell + sc) % TILE - cell + TILE * shift_col
                rho2 = spacing * spacing * (dr[:, None] ** 2 + dc[None, :] ** 2)
                radius = np.sqrt(rho2 + lift_height**2)
                green = np.exp(1j * wave_number * radius) / radius
                log_slope = 1j * wave_number - 1 / radius
                first_r = green * log_slope
                second_r = green * (log_slope**2 + 1 / radius**2)
                rise = lift_height / radius
                k1 = first_r * rise
                k2 = 0.5 * (second_r * rise**2 + first_r * (1 - rise**2) / radius)
                a0 = green - lift_height * k1 + lift_height**2 * k2
                a1 = k1 - 2 * lift_height * k2
                offset = rho2 - X_TOP / 2
                line = SIN_FIT[-2] - k2.imag
                level = SIN_FIT[-1] - a0.imag + k2.imag * offset
                entry = [offset, a0.real, a1.real, k2.real, level, line, a1.imag]
                entries.append([np.tile(e, (ROWS // TILE, LANES // TILE)) for e in entry])
    return np.asarray(entries, np.float32)


SIDE_KINDS = ((0, 0), (0, -1), (0, 1))
OVER_KINDS = ((-1, 0), (1, 0))
SIDE_TABLE = near_table(SIDE_KINDS)
OVER_TABLE = near_table(OVER_KINDS)


def horner(coefficients, x):
    total = coefficients[0] * x + coefficients[1]
    for c in coefficients[2:]:
        total = total * x + c
    return total


def turned_index(axis, turn):
    place = lax.broadcasted_iota(jnp.int32, (ROWS, LANES), axis)
    within = place % TILE
    return place - within + (within + turn) % TILE


def turn_cells(x, axis, turn):
    if turn == 0:
        return x
    return jnp.take_along_axis(x, turned_index(axis, turn), axis=axis)


def meet(raised, source, table_ref, entry):
    real, imag, height = source
    w = raised - height
    v = w * w
    u = v + table_ref[entry, 0]
    root = lax.rsqrt(u + X_TOP / 2)
    gap_real = horner(COS_FIT, u) * root - (
        table_ref[entry, 2] * w + (table_ref[entry, 3] * v + table_ref[entry, 1])
    )
    fitted = (horner(SIN_FIT[:-2], u) * u + table_ref[entry, 5]) * u + table_ref[entry, 4]
    gap_imag = fitted - table_ref[entry, 6] * w
    return gap_real * real - gap_imag * imag, gap_real * imag + gap_imag * real


def meet_tiles(raised, sources, table_ref):
    total_real = jnp.zeros((ROWS, LANES), jnp.float32)
    total_imag = jnp.zeros((ROWS, LANES), jnp.float32)
    for kind, source in enumerate(sources):
        for sc in range(TILE):
            column = [turn_cells(x, 1, sc) for x in source]
            for sr in range(TILE):
                cells = [turn_cells(x, 0, sr) for x in column]
                entry = (kind * TILE + sr) * TILE + sc
                real, imag = meet(raised, cells, table_ref, entry)
                total_real = total_real + real
                total_imag = total_imag + imag
    return total_real, total_imag


def spread_kernel(
    flat_ref,
    slope_ref,
    curve_ref,
    twist_ref,
    small_ref,
    after_ref,
    spread_ref,
    twist_out,
    small_out,
    lined,
    sems,
):
    copies = fetch(
        [
            (flat_ref, lined.at[0]),
            (slope_ref, lined.at[1]),
            (curve_ref, lined.at[2]),
            (twist_ref, twist_out),
            (small_ref, small_out),
        ],
        sems,
    )
    for copy in copies:
        copy.wait()
    spread_spectra([lined.at[m] for m in range(3)], spread_ref)


def side_kernel(
    own_ref,
    far_ref,
    mate_ref,
    diag_ref,
    table_ref,
    back_twist_ref,
    back_last_ref,
    after_ref,
    out_ref,
    back_twist_out,
    back_last_out,
    edge,
    sems,
):
    q = lax.axis_index("gy")
    copies = fetch(
        [(back_twist_ref.at[q], back_twist_out), (back_last_ref.at[q], back_last_out)], sems
    )
    odd = q % 2 == 1
    for part in range(3):
        last = slice(SPAN - LANES, SPAN)
        first = slice(0, LANES)
        edge[0, part] = jnp.where(odd, mate_ref[part, :, last], diag_ref[part, :, last])
        edge[SUBS + 1, part] = jnp.where(odd, diag_ref[part, :, first], mate_ref[part, :, first])
        for n in range(SUBS):
            edge[n + 1, part] = own_ref[part, :, LANES * n : LANES * (n + 1)]
    lane = lax.broadcasted_iota(jnp.int32, (ROWS, LANES), 1)

    for n in range(SUBS):
        before = [edge[n, part] for part in range(3)]
        here = [edge[n + 1, part] for part in range(3)]
        after = [edge[n + 2, part] for part in range(3)]
        left = [
            jnp.where(lane < TILE, pltpu.roll(x, TILE, 1), pltpu.roll(y, TILE, 1))
            for x, y in zip(before, here)
        ]
        right = [
            jnp.where(
                lane < LANES - TILE,
                pltpu.roll(y, LANES - TILE, 1),
                pltpu.roll(z, LANES - TILE, 1),
            )
            for y, z in zip(here, after)
        ]
        real, imag = meet_tiles(here[2] + lift_height, (here, left, right), table_ref)
        out_ref[0, :, LANES * n : LANES * (n + 1)] = area_weight * real
        out_ref[1, :, LANES * n : LANES * (n + 1)] = area_weight * imag
    for copy in copies:
        copy.wait()


def over_kernel(own_ref, up_ref, down_ref, table_ref, side_ref, same_ref, mate_ref, out_ref):
    for n in range(SUBS):
        lanes = slice(LANES * n, LANES * (n + 1))
        here = [own_ref[part, :, lanes] for part in range(3)]
        above = [
            jnp.concatenate([up_ref[part, :, lanes], here[part][:TILE]], 0) for part in range(3)
        ]
        below = [
            jnp.concatenate([here[part][TILE:], down_ref[part, :, lanes]], 0) for part in range(3)
        ]
        real, imag = meet_tiles(here[2] + lift_height, (above, below), table_ref)
        for part, near in enumerate((real, imag)):
            spectral = same_ref[0, part, :, lanes] + mate_ref[0, part, :, lanes]
            out_ref[part, :, lanes] = spectral + (side_ref[part, :, lanes] + area_weight * near)


def all_to_all_x(messages):
    shaped = messages.reshape(DEV_X, 1, 3 * LANES)
    moved = lax.all_to_all(shaped, "gx", split_axis=0, concat_axis=0, tiled=True)
    return moved.reshape(3 * DEV_X, LANES)


def local(unknown, height, spectrum_flat, spectrum_slope, spectrum_curve):
    mate_pairs = [(g, g ^ 1) for g in range(DEV_Y)]
    far_pairs = [(g, g ^ 2) for g in range(DEV_Y)]
    own, row_first, row_twist, outer = call(
        pack_kernel,
        (
            f32(3, ROWS, SPAN),
            held(2, LANES, LANES),
            held(2, HALF, LANES),
            held(2, LANES, 2 * LANES),
        ),
        unknown,
        height,
        TABLES["row_first"],
        TABLES["row_twist"],
        TABLES["outer"],
        loose=5,
        scratch=[pltpu.SemaphoreType.DMA((5,))],
    )
    far = lax.ppermute(own, "gy", far_pairs)
    mate = lax.ppermute(own, "gy", mate_pairs)
    diagonal = lax.ppermute(far, "gy", mate_pairs)
    groups = (own, far, mate, diagonal)
    sent, low = call(
        row_kernel,
        (f32(3 * DEV_X, LANES), f32(3, TILE, SPAN)),
        *groups,
        row_first,
        row_twist,
        outer,
    )
    arrived = all_to_all_x(sent)
    lined = [
        s.reshape(2, 64, LANES).transpose(1, 0, 2).reshape(2 * 64, LANES)
        for s in (spectrum_flat, spectrum_slope, spectrum_curve)
    ]
    spread, col_twist, col_small = call(
        spread_kernel,
        (
            held(6, LANES, LANES),
            held(2, LANES, LANES),
            held(2, 2, LANES, LANES),
        ),
        *lined,
        TABLES["col_twist"],
        TABLES["col_small"],
        sent,
        loose=5,
        waits=1,
        scratch=[
            pltpu.VMEM((3, LANES, LANES), jnp.float32),
            pltpu.SemaphoreType.DMA((5,)),
        ],
        flops=10_000_000,
    )
    up = lax.ppermute(low, "gx", [(i, (i + 1) % DEV_X) for i in range(DEV_X)])
    side, back_twist, back_last = call(
        side_kernel,
        (held(2, ROWS, SPAN), held(2, LANES, LANES), held(2, LANES, LANES)),
        *groups,
        SIDE_TABLE,
        TABLES["back_twist"],
        TABLES["back_last"],
        spread,
        loose=2,
        waits=1,
        scratch=[
            pltpu.VMEM((SUBS + 2, 3, ROWS, LANES), jnp.float32),
            pltpu.SemaphoreType.DMA((2,)),
        ],
        flops=30_000_000,
    )
    back, high = call(
        column_kernel,
        (f32(3 * DEV_X, LANES), f32(3, TILE, SPAN)),
        arrived,
        spread,
        outer,
        col_twist,
        col_small,
        own,
        side,
        waits=1,
    )
    down = lax.ppermute(high, "gx", [((i + 1) % DEV_X, i) for i in range(DEV_X)])
    returned = all_to_all_x(back)
    same, crossed = call(
        inverse_kernel,
        (f32(2, 2, ROWS, SPAN), f32(2, 2, ROWS, SPAN)),
        returned,
        *groups,
        outer,
        back_twist,
        back_last,
        up,
        down,
        waits=2,
    )
    from_mate = lax.ppermute(crossed, "gy", mate_pairs)
    from_far = lax.ppermute(same[1] + from_mate[1], "gy", far_pairs)
    base = call(
        over_kernel,
        f32(2, ROWS, SPAN),
        own,
        up,
        down,
        OVER_TABLE,
        side,
        same,
        from_mate,
        flops=20_000_000,
    )
    return base + from_far


def solution(mesh):
    return jax.shard_map(
        local,
        mesh=mesh,
        in_specs=(
            P(None, "gx", "gy"),
            P("gx", "gy"),
            P(None, ("gx", "gy")),
            P(None, ("gx", "gy")),
            P(None, ("gx", "gy")),
        ),
        out_specs=P(None, "gx", "gy"),
        check_vma=False,
    )
```
